32 devices in a mesh: freq: 8 (over z, x), tile: 4 (over y, core).
Axes of the slice: x: 2, y: 2, z: 4, core: 2. Of those that a mesh axis runs over, the one named last changes fastest.
Arguments:
- sky_cube: float32 [32, 64, 128], P(('freq', 'tile')), may hold values from -6 to 6
- kernel_one: bfloat16 [8, 1, 3, 3, 3], replicated, may hold values from -1.25 to 1.25
- bias_one: float32 [8], replicated, may hold values from -2 to 2
- kernel_two: bfloat16 [8, 8, 3, 3, 3], replicated, may hold values from -0.4375 to 0.4375
- bias_two: float32 [8], replicated, may hold values from -2 to 2
- kernel_three: bfloat16 [16, 8, 3, 3, 3], replicated, may hold values from -0.4375 to 0.4375
- bias_three: float32 [16], replicated, may hold values from -2 to 2
Outputs:
- features: bfloat16 [16, 16, 32, 64], P(None, 'freq', 'tile')
The draws below stay inside these ranges and needn't reach their ends.
All inputs are finite; a program needn't handle non-finite values.
Results may differ from the reference program's by a relative error of at most 0.0066.
Values may be sent and summed in bfloat16 or wider, within the bound.
No kernel may reach another device: no remote copies, remote signals or barrier semaphores. Data moves between devices by JAX's collectives and lax.ppermute only.
A program may use at most 64 MiB of HBM per device.

```python
import jax
import jax.numpy as jnp
from jax import lax

NX = 128
C1 = 8
C2 = 8
C3 = 16
GROUP = 4
CH = 32
NY = 64
N_FREQ = 8


def level_of(own_key, dims, pieces, low, largest):
    level = 1.0
    for axis_at, shards_of in pieces:
        heights = jax.random.uniform(jax.random.fold_in(jax.random.fold_in(own_key, 6), axis_at), (shards_of,), jnp.float32, low / len(pieces), largest / len(pieces))
        level = level * jnp.repeat(jnp.exp(heights), dims[axis_at] // shards_of).reshape((-1,) + (1,) * (len(dims) - 1 - axis_at))
    return level


def centred(stream_key, extent, deviation, reach, shards=(), held_as=jnp.bfloat16):
    entries = deviation * jax.random.normal(stream_key, extent, jnp.float32)
    if shards:
        entries = entries * level_of(stream_key, extent, shards, -0.22, 0.18)
    return jnp.clip(entries, -reach, reach).astype(held_as)


def setup_inputs(seed: int = 0) -> dict:
    arg_keys = jax.random.split(jax.random.key(seed), 8)
    return {
        "sky_cube": centred(arg_keys[0], (CH, NY, NX), 1.0, 6.0, ((0, 32),), jnp.float32),
        "kernel_one": centred(arg_keys[1], (C1, 1, 3, 3, 3), 27 ** -0.5, 1.25),
        "bias_one": centred(arg_keys[2], (C1,), 0.4, 2.0, (), jnp.float32),
        "kernel_two": centred(arg_keys[3], (C2, C1, 3, 3, 3), (27 * C1) ** -0.5, 0.4375),
        "bias_two": centred(arg_keys[4], (C2,), 0.4, 2.0, (), jnp.float32),
        "kernel_three": centred(arg_keys[5], (C3, C2, 3, 3, 3), (27 * C2) ** -0.5, 0.4375),
        "bias_three": centred(arg_keys[6], (C3,), 0.4, 2.0, (), jnp.float32),
    }


def convolve(volume, kernel, strides, padding):
    result = lax.conv_general_dilated(volume[None], kernel, strides, padding, dimension_numbers=("NCDHW", "OIDHW", "NCDHW"), preferred_element_type=jnp.float32)
    return result[0]


def leaky_relu(values):
    return jnp.maximum(values, 0.1 * values)


def reference(sky_cube, kernel_one, bias_one, kernel_two, bias_two, kernel_three, bias_three):
    slab = sky_cube.astype(jnp.bfloat16)
    padded = jnp.pad(slab, ((3, 3), (0, 0), (0, 0)))
    same_rows = ((0, 0), (1, 1), (1, 1))

    def one_group(index):
        begin_at = (index * GROUP).astype(jnp.int32)
        section = lax.dynamic_slice_in_dim(padded, begin_at, GROUP + 6, 0)[None]
        planes = begin_at - 2 + jnp.arange(GROUP + 4, dtype=jnp.int32)
        inside = ((planes >= 0) & (planes < CH))[None, :, None, None]
        values = leaky_relu(convolve(section, kernel_one, (1, 1, 1), same_rows) + bias_one[:, None, None, None])
        layer_one = jnp.where(inside, values, 0.0).astype(jnp.bfloat16)
        planes = begin_at - 1 + jnp.arange(GROUP + 2, dtype=jnp.int32)
        inside = ((planes >= 0) & (planes < CH))[None, :, None, None]
        values = leaky_relu(convolve(layer_one, kernel_two, (1, 1, 1), same_rows) + bias_two[:, None, None, None])
        layer_two = jnp.where(inside, values, 0.0).astype(jnp.bfloat16)
        values = leaky_relu(convolve(layer_two[:, :GROUP + 1], kernel_three, (2, 2, 2), same_rows) + bias_three[:, None, None, None])
        return values.astype(jnp.bfloat16)

    stacked = lax.map(one_group, jnp.arange(N_FREQ).astype(jnp.int32))
    return jnp.transpose(stacked, (1, 0, 2, 3, 4)).reshape(C3, CH // 2, NY // 2, NX // 2)
```

```python
import functools

import jax
import jax.numpy as jnp
from jax import lax
from jax.experimental import pallas as pl
from jax.experimental.pallas import tpu as pltpu
from jax.sharding import PartitionSpec as P

BF = jnp.bfloat16
F32 = jnp.float32
VM = pl.BlockSpec(memory_space=pltpu.VMEM)
SM = pl.BlockSpec(memory_space=pltpu.SMEM)


def even(n):
    return n + n % 2


def up_to(n, unit):
    return -(-n // unit) * unit


class Plan:
    def __init__(self, strip, c1, c2, c3):
        self.strip, self.c1, self.c2, self.c3 = strip, c1, c2, c3
        self.slots = strip + 8
        self.plane_k = up_to(3 * self.slots, 16)
        self.k1 = up_to(3 * self.plane_k, 256)
        self.r1 = even(strip + 3)
        self.r2 = even(strip + 1)
        self.r3 = strip // 2
        self.k2 = up_to(3 * self.r1 * c1, 256)
        self.k3 = up_to(3 * self.r2 * c2, 256)


def leaky_relu(values):
    return jnp.maximum(values, 0.1 * values)


def column_of(bias_ref, rows, lanes):
    at = lax.broadcasted_iota(jnp.int32, (rows, lanes), 0)
    out = jnp.zeros((rows, lanes), F32)
    for o in range(rows):
        out = jnp.where(at == o, bias_ref[o], out)
    return out


def bands_kernel(plan, bias1, bias2, bias3, base1, base2, base3, t1, t2, t3, b1, b2, b3):
    c1, c2, c3 = plan.c1, plan.c2, plan.c3
    slots = plan.slots
    b1[...] = column_of(bias1, c1, 128)
    b2[...] = column_of(bias2, c2, 128)
    lanes = lax.broadcasted_iota(jnp.int32, (c1, plan.k1), 1)
    slot = lax.rem(lax.rem(lanes, plan.plane_k), slots)
    taps = [jnp.where(slot == b, base1[...], 0.0) for b in range(3)]

    def rolled(x, by):
        return pltpu.roll(x, by, 1) if by else x

    def tap_at(b, to):
        return rolled(taps[b], (to - b) % plan.k1)

    for y in range(0, plan.r1, 2):
        rows = [sum(tap_at(b, (row - 3 + b) % slots) for b in range(3)) for row in (y, y + 1)]
        t1[y * c1 : (y + 2) * c1, :] = jnp.concatenate(rows, axis=0).astype(BF)
    for a in range(3):
        base = base2[a]
        for y in range(0, plan.r2, 2):
            rows = [rolled(base, (y + k) * c1) for k in range(2)]
            t2[a, y * c2 : (y + 2) * c2, :] = jnp.concatenate(rows, axis=0).astype(BF)
    n3 = plan.r3 * c3
    row = lax.broadcasted_iota(jnp.int32, (n3, n3), 0)
    col = lax.broadcasted_iota(jnp.int32, (n3, n3), 1)
    turn = ((row // plan.r3 == col % c3) & (row % plan.r3 == col // c3)).astype(F32).astype(BF)
    for a in range(3):
        base = base3[a]
        rows = [rolled(base, 2 * y * c2) for y in range(plan.r3)]
        stacked = jnp.concatenate(rows, axis=0).astype(BF)
        t3[a] = jnp.dot(turn, stacked, preferred_element_type=F32).astype(BF)
    for o in range(c3):
        b3[o * plan.r3 : (o + 1) * plan.r3, :] = jnp.full((plan.r3, 128), bias3[o], F32)


def layers_kernel(plan, depth, own, got, other, t1, t2, t3, b1, b2, b3, out, x2, x3):
    freq, tile = lax.axis_index("freq"), lax.axis_index("tile")
    last_group, last_strip = lax.axis_size("freq") - 1, lax.axis_size("tile") - 1
    strip, c1, c2 = plan.strip, plan.c1, plan.c2
    here = pl.multiple_of(tile * strip, 16)
    above = pl.multiple_of(jnp.maximum(tile - 1, 0) * strip + strip - 16, 16)
    below = pl.multiple_of(jnp.minimum(tile + 1, last_strip) * strip, 16)
    has_above, has_below = tile > 0, tile < last_strip
    has_lower, has_upper = freq > 0, freq < last_group
    upward = lax.rem(tile, 2) == 0

    sub = lax.broadcasted_iota(jnp.int32, (8, 128), 0)
    rim_keep = ((sub < 4) & has_below) | ((sub >= 4) & has_above)

    def lane_of(rows):
        return lax.broadcasted_iota(jnp.int32, (rows, 128), 1)

    def window(ref, plane):
        middle = ref[plane, pl.ds(here, strip), :].astype(F32)
        rim_above = ref[plane, pl.ds(above, 16), :].astype(F32)[8:]
        rim_below = ref[plane, pl.ds(below, 16), :].astype(F32)[:8]
        rim = jnp.where(rim_keep, jnp.where(sub < 4, rim_below, rim_above), 0.0)
        return jnp.concatenate([middle, rim], axis=0)

    def shifted(x):
        lane = lane_of(x.shape[0])
        return (
            jnp.where(lane == 0, 0.0, pltpu.roll(x, 1, 1)),
            x,
            jnp.where(lane == 127, 0.0, pltpu.roll(x, 127, 1)),
        )

    slab = []
    for p in range(depth - 3, depth):
        rows = jnp.where(upward, window(got, p), window(other, p))
        slab.append(jnp.where(has_lower, rows, 0.0))
    for p in range(depth):
        slab.append(window(own, p))
    for p in range(2):
        rows = jnp.where(upward, window(other, p), window(got, p))
        slab.append(jnp.where(has_upper, rows, 0.0))
    pad = jnp.zeros((plan.plane_k - 3 * plan.slots, 128), F32)
    pieces = [jnp.concatenate([*shifted(rows), pad], axis=0).astype(BF) for rows in slab]

    k1_pad = jnp.zeros((plan.k1 - 3 * plan.plane_k, 128), BF)
    n1, n2 = plan.r1 * c1, plan.r2 * c2
    planes1, planes2 = depth + 3, depth + 1
    x2[3 * n1 :, :] = jnp.zeros((plan.k2 - 3 * n1, planes1 * 128), BF)
    x3[3 * n2 :, :] = jnp.zeros((plan.k3 - 3 * n2, planes2 * 128), BF)

    def chunks(count):
        return [range(p, min(p + 2, count)) for p in range(0, count, 2)]

    for chunk in chunks(planes1):
        x1 = jnp.concatenate(
            [jnp.concatenate([*pieces[p : p + 3], k1_pad], axis=0) for p in chunk], axis=1
        )
        sums = jnp.dot(t1[...], x1, preferred_element_type=F32)
        for i, p in enumerate(chunk):
            v = sums[:, i * 128 : (i + 1) * 128].reshape(plan.r1, c1, 128)
            v = leaky_relu(v + b1[...])
            if p < 2:
                v = jnp.where(has_lower, v, 0.0)
            if p == planes1 - 1:
                v = jnp.where(has_upper, v, 0.0)
            v = jnp.concatenate(
                [
                    jnp.where(has_above, v[:2], 0.0),
                    v[2 : strip + 2],
                    jnp.where(has_below, v[strip + 2 :], 0.0),
                ],
                axis=0,
            ).reshape(n1, 128)
            for c, rows in enumerate(shifted(v)):
                x2[c * n1 : (c + 1) * n1, p * 128 : (p + 1) * 128] = rows.astype(BF)

    for chunk in chunks(planes2):
        sums = sum(
            jnp.dot(
                t2[a],
                x2[:, (chunk[0] + a) * 128 : (chunk[-1] + a + 1) * 128],
                preferred_element_type=F32,
            )
            for a in range(3)
        )
        for i, p in enumerate(chunk):
            v = sums[:, i * 128 : (i + 1) * 128].reshape(plan.r2, c2, 128)
            v = leaky_relu(v + b2[...])
            if p == 0:
                v = jnp.where(has_lower, v, 0.0)
            v = jnp.concatenate([jnp.where(has_above, v[:1], 0.0), v[1:]], axis=0).reshape(n2, 128)
            for c, rows in enumerate(shifted(v)):
                x3[c * n2 : (c + 1) * n2, p * 128 : (p + 1) * 128] = rows.astype(BF)

    pick = (
        lax.broadcasted_iota(jnp.int32, (128, 64), 0)
        == 2 * lax.broadcasted_iota(jnp.int32, (128, 64), 1)
    ).astype(F32).astype(BF)
    for f in range(0, depth // 2, 2):
        pair = range(f, min(f + 2, depth // 2))
        sums = 0.0
        for a in range(3):
            x = jnp.concatenate([x3[:, (2 * k + a) * 128 : (2 * k + a + 1) * 128] for k in pair], axis=1)
            sums = sums + jnp.dot(t3[a], x, preferred_element_type=F32)
        for i, k in enumerate(pair):
            v = leaky_relu(sums[:, i * 128 : (i + 1) * 128] + b3[...]).astype(BF)
            v = jnp.dot(v, pick, preferred_element_type=F32)
            out[:, k] = v.reshape(plan.c3, plan.r3, 64).astype(BF)


def band_base(kernel, rows, k):
    out_channels, in_channels = kernel.shape[:2]
    base = jnp.transpose(kernel.astype(F32), (2, 0, 4, 3, 1))
    base = jnp.pad(base, ((0, 0), (0, 0), (0, 0), (0, rows - 3), (0, 0)))
    base = base.reshape(3, out_channels, 3 * rows * in_channels)
    return jnp.pad(base, ((0, 0), (0, 0), (0, k - base.shape[2])))


def body(sky_cube, kernel_one, bias_one, kernel_two, bias_two, kernel_three, bias_three):
    tiles, groups = lax.axis_size("tile"), lax.axis_size("freq")
    strip = sky_cube.shape[1] // tiles
    depth = tiles * sky_cube.shape[0]
    c1, c2, c3 = (kernel.shape[0] for kernel in (kernel_one, kernel_two, kernel_three))
    plan = Plan(strip, c1, c2, c3)

    own = lax.all_gather(sky_cube.astype(BF), "tile", axis=0, tiled=True)
    pairs = []
    for g in range(groups):
        for t in range(tiles):
            to = g + 1 if t % 2 == 0 else g - 1
            target = to * tiles + t if 0 <= to < groups else g * tiles + (t ^ 1)
            pairs.append((g * tiles + t, target))
    got = lax.ppermute(own, ("freq", "tile"), pairs)
    other = lax.ppermute(got, "tile", [(t, t ^ 1) for t in range(tiles)])

    base1 = jnp.transpose(kernel_one[:, 0].astype(F32), (0, 1, 3, 2))
    base1 = jnp.pad(base1, ((0, 0), (0, 0), (0, 0), (0, plan.slots - 3)))
    base1 = base1.reshape(c1, 3, 3 * plan.slots)
    base1 = jnp.pad(base1, ((0, 0), (0, 0), (0, plan.plane_k - 3 * plan.slots)))
    base1 = base1.reshape(c1, 3 * plan.plane_k)
    base1 = jnp.pad(base1, ((0, 0), (0, plan.k1 - 3 * plan.plane_k)))
    base2 = band_base(kernel_two, plan.r1, plan.k2)
    base3 = band_base(kernel_three, plan.r2, plan.k3)

    bands = pl.pallas_call(
        functools.partial(bands_kernel, plan),
        name="bands",
        out_shape=[
            jax.ShapeDtypeStruct((plan.r1 * c1, plan.k1), BF),
            jax.ShapeDtypeStruct((3, plan.r2 * c2, plan.k2), BF),
            jax.ShapeDtypeStruct((3, plan.r3 * c3, plan.k3), BF),
            jax.ShapeDtypeStruct((c1, 128), F32),
            jax.ShapeDtypeStruct((c2, 128), F32),
            jax.ShapeDtypeStruct((plan.r3 * c3, 128), F32),
        ],
        in_specs=[SM] * 3 + [VM] * 3,
        out_specs=[VM] * 6,
        compiler_params=pltpu.CompilerParams(vmem_limit_bytes=32 * 2**20),
    )(bias_one, bias_two, bias_three, base1, base2, base3)

    return pl.pallas_call(
        functools.partial(layers_kernel, plan, depth),
        name="layers",
        out_shape=jax.ShapeDtypeStruct((c3, depth // 2, plan.r3, sky_cube.shape[2] // 2), BF),
        in_specs=[VM] * 9,
        out_specs=VM,
        scratch_shapes=[
            pltpu.VMEM((plan.k2, (depth + 3) * 128), BF),
            pltpu.VMEM((plan.k3, (depth + 1) * 128), BF),
        ],
        compiler_params=pltpu.CompilerParams(vmem_limit_bytes=32 * 2**20),
    )(own, got, other, *bands)


def solution(mesh):
    return jax.shard_map(
        body,
        mesh=mesh,
        in_specs=(P(("freq", "tile"), None, None), P(), P(), P(), P(), P(), P()),
        out_specs=P(None, "freq", "tile", None),
        check_vma=False,
    )
```

```python
import functools

import jax
import jax.numpy as jnp
from jax import lax
from jax.experimental import pallas as pl
from jax.experimental.pallas import tpu as pltpu
from jax.sharding import PartitionSpec as P

BF = jnp.bfloat16
F32 = jnp.float32
VM = pl.BlockSpec(memory_space=pltpu.VMEM)
SM = pl.BlockSpec(memory_space=pltpu.SMEM)


def even(n):
    return n + n % 2


def up_to(n, unit):
    return -(-n // unit) * unit


class Plan:
    def __init__(self, strip, c1, c2, c3):
        self.strip, self.c1, self.c2, self.c3 = strip, c1, c2, c3
        self.slots = strip + 8
        self.plane_k = up_to(3 * self.slots, 16)
        self.k1 = up_to(3 * self.plane_k, 256)
        self.r1 = even(strip + 3)
        self.r2 = even(strip + 1)
        self.r3 = strip // 2
        self.k2 = up_to(3 * self.r1 * c1, 256)
        self.k3 = up_to(3 * self.r2 * c2, 256)


def leaky_relu(values):
    return jnp.maximum(values, 0.1 * values)


def column_of(bias_ref, rows, lanes):
    at = lax.broadcasted_iota(jnp.int32, (rows, lanes), 0)
    out = jnp.zeros((rows, lanes), F32)
    for o in range(rows):
        out = jnp.where(at == o, bias_ref[o], out)
    return out


def ones_where(hit):
    return hit.astype(F32).astype(BF)


def dot_over_rows(left, right):
    return lax.dot_general(left, right, (((0,), (0,)), ((), ())), preferred_element_type=F32)


def rolled(x, by):
    return pltpu.roll(x, by, 1) if by else x


def bands_12_kernel(plan, bias1, bias2, w1, w2, t1, t2, b1, b2):
    c1, c2 = plan.c1, plan.c2
    slots = plan.slots
    b1[...] = column_of(bias1, c1, 128)
    b2[...] = column_of(bias2, c2, 128)
    tap = lax.broadcasted_iota(jnp.int32, (3, plan.k1), 0)
    lane = lax.broadcasted_iota(jnp.int32, (3, plan.k1), 1)
    taps = []
    for b in range(3):
        taps.append(
            sum(
                dot_over_rows(w1[a, b], ones_where(lane == a * plan.plane_k + tap * slots))
                for a in range(3)
            )
        )
    for y in range(0, plan.r1, 2):
        rows = [
            sum(rolled(taps[b], (row - 3 + b) % slots) for b in range(3)) for row in (y, y + 1)
        ]
        t1[y * c1 : (y + 2) * c1, :] = jnp.concatenate(rows, axis=0).astype(BF)

    for a in range(3):
        parts = [jnp.zeros((c2, 128), F32) for _ in range(plan.k2 // 128)]
        for b in range(3):
            for c in range(3):
                at = (c * plan.r1 + b) * c1
                tile = w2[a, b, c].astype(F32)
                tile = jnp.concatenate([tile, jnp.zeros((c2, 128 - c1), F32)], axis=1)
                parts[at // 128] += rolled(tile, at % 128)
        base = jnp.concatenate(parts, axis=1)
        for y in range(0, plan.r2, 2):
            rows = [rolled(base, (y + k) * c1) for k in range(2)]
            t2[a, y * c2 : (y + 2) * c2, :] = jnp.concatenate(rows, axis=0).astype(BF)


def bands_3_kernel(plan, bias3, w3, t3, b3):
    c2, c3 = plan.c2, plan.c3
    for o in range(c3):
        b3[o * plan.r3 : (o + 1) * plan.r3, :] = jnp.full((plan.r3, 128), bias3[o], F32)
    n3 = plan.r3 * c3
    row = lax.broadcasted_iota(jnp.int32, (n3, n3), 0)
    col = lax.broadcasted_iota(jnp.int32, (n3, n3), 1)
    turn = ones_where((row // plan.r3 == col % c3) & (row % plan.r3 == col // c3))
    row = lax.broadcasted_iota(jnp.int32, (9 * c2, plan.k3), 0)
    lane = lax.broadcasted_iota(jnp.int32, (9 * c2, plan.k3), 1)
    b, c, i = row // (3 * c2), (row // c2) % 3, row % c2
    spread = ones_where(lane == (c * plan.r2 + b) * c2 + i)
    for a in range(3):
        taken = w3[a].astype(F32).reshape(9 * c2, c3).astype(BF)
        base = dot_over_rows(taken, spread)
        rows = [rolled(base, 2 * y * c2) for y in range(plan.r3)]
        stacked = jnp.concatenate(rows, axis=0).astype(BF)
        t3[a] = jnp.dot(turn, stacked, preferred_element_type=F32).astype(BF)


def layers_kernel(plan, depth, span, own, got, other, t1, t2, b1, b2, t3, b3, out, x2, x3):
    freq, tile = lax.axis_index("freq"), lax.axis_index("tile")
    last_group, last_strip = lax.axis_size("freq") - 1, lax.axis_size("tile") - 1
    strip, c1, c2 = plan.strip, plan.c1, plan.c2
    here = tile * strip
    above = jnp.maximum(tile - 1, 0) * strip + strip - 16
    below = jnp.minimum(tile + 1, last_strip) * strip
    first = first_row(plan, tile, last_strip + 1, span)
    has_above, has_below = tile > 0, tile < last_strip
    has_lower, has_upper = freq > 0, freq < last_group
    from_lower = lax.rem(tile, 2) == 1

    sub = lax.broadcasted_iota(jnp.int32, (8, 128), 0)
    rim_keep = ((sub < 4) & has_below) | ((sub >= 4) & has_above)

    def lane_of(rows):
        return lax.broadcasted_iota(jnp.int32, (rows, 128), 1)

    def window(ref, plane, first=first):
        def rows(at, count):
            at = jnp.clip(at - first, 0, ref.shape[1] - count)
            return ref[plane, pl.ds(pl.multiple_of(at, 16), count), :].astype(F32)

        middle = rows(here, strip)
        rim_above = rows(above, 16)[8:]
        rim_below = rows(below, 16)[:8]
        rim = jnp.where(rim_keep, jnp.where(sub < 4, rim_below, rim_above), 0.0)
        return jnp.concatenate([middle, rim], axis=0)

    def shifted(x):
        lane = lane_of(x.shape[0])
        return (
            jnp.where(lane == 0, 0.0, pltpu.roll(x, 1, 1)),
            x,
            jnp.where(lane == 127, 0.0, pltpu.roll(x, 127, 1)),
        )

    slab = []
    for p in range(3):
        rows = jnp.where(from_lower, window(got, p), window(other, p))
        slab.append(jnp.where(has_lower, rows, 0.0))
    for p in range(depth):
        slab.append(window(own, p, 0))
    for p in range(2):
        rows = jnp.where(from_lower, window(other, p), window(got, p))
        slab.append(jnp.where(has_upper, rows, 0.0))
    pad = jnp.zeros((plan.plane_k - 3 * plan.slots, 128), F32)
    pieces = [jnp.concatenate([*shifted(rows), pad], axis=0).astype(BF) for rows in slab]

    k1_pad = jnp.zeros((plan.k1 - 3 * plan.plane_k, 128), BF)
    n1, n2 = plan.r1 * c1, plan.r2 * c2
    planes1, planes2 = depth + 3, depth + 1
    x2[3 * n1 :, :] = jnp.zeros((plan.k2 - 3 * n1, planes1 * 128), BF)
    x3[3 * n2 :, :] = jnp.zeros((plan.k3 - 3 * n2, planes2 * 128), BF)

    def chunks(count):
        return [range(p, min(p + 2, count)) for p in range(0, count, 2)]

    for chunk in chunks(planes1):
        x1 = jnp.concatenate(
            [jnp.concatenate([*pieces[p : p + 3], k1_pad], axis=0) for p in chunk], axis=1
        )
        sums = jnp.dot(t1[...], x1, preferred_element_type=F32)
        for i, p in enumerate(chunk):
            v = sums[:, i * 128 : (i + 1) * 128].reshape(plan.r1, c1, 128)
            v = leaky_relu(v + b1[...])
            if p < 2:
                v = jnp.where(has_lower, v, 0.0)
            if p == planes1 - 1:
                v = jnp.where(has_upper, v, 0.0)
            v = jnp.concatenate(
                [
                    jnp.where(has_above, v[:2], 0.0),
                    v[2 : strip + 2],
                    jnp.where(has_below, v[strip + 2 :], 0.0),
                ],
                axis=0,
            ).reshape(n1, 128)
            for c, rows in enumerate(shifted(v)):
                x2[c * n1 : (c + 1) * n1, p * 128 : (p + 1) * 128] = rows.astype(BF)

    for chunk in chunks(planes2):
        sums = sum(
            jnp.dot(
                t2[a],
                x2[:, (chunk[0] + a) * 128 : (chunk[-1] + a + 1) * 128],
                preferred_element_type=F32,
            )
            for a in range(3)
        )
        for i, p in enumerate(chunk):
            v = sums[:, i * 128 : (i + 1) * 128].reshape(plan.r2, c2, 128)
            v = leaky_relu(v + b2[...])
            if p == 0:
                v = jnp.where(has_lower, v, 0.0)
            v = jnp.concatenate([jnp.where(has_above, v[:1], 0.0), v[1:]], axis=0).reshape(n2, 128)
            for c, rows in enumerate(shifted(v)):
                x3[c * n2 : (c + 1) * n2, p * 128 : (p + 1) * 128] = rows.astype(BF)

    pick = (
        lax.broadcasted_iota(jnp.int32, (128, 64), 0)
        == 2 * lax.broadcasted_iota(jnp.int32, (128, 64), 1)
    ).astype(F32).astype(BF)
    for f in range(0, depth // 2, 2):
        pair = range(f, min(f + 2, depth // 2))
        sums = 0.0
        for a in range(3):
            x = jnp.concatenate([x3[:, (2 * k + a) * 128 : (2 * k + a + 1) * 128] for k in pair], axis=1)
            sums = sums + jnp.dot(t3[a], x, preferred_element_type=F32)
        for i, k in enumerate(pair):
            v = leaky_relu(sums[:, i * 128 : (i + 1) * 128] + b3[...]).astype(BF)
            v = jnp.dot(v, pick, preferred_element_type=F32)
            out[:, k] = v.reshape(plan.c3, plan.r3, 64).astype(BF)


def first_row(plan, tile, tiles, span):
    return jnp.clip((tile // 2) * 2 * plan.strip - 16, 0, tiles * plan.strip - span)


def gathered(plane, tiles):
    if tiles & (tiles - 1):
        return lax.all_gather(plane.astype(BF), "tile", axis=0, tiled=True)
    tile, size, held = lax.axis_index("tile"), 1, plane
    while size < tiles:
        taken = lax.ppermute(held, "tile", [(t, t ^ (2 * size - 1)) for t in range(tiles)])
        if size == 1:
            taken = lax.optimization_barrier(taken).astype(BF)
            held = held.astype(BF)
        upper = (tile // size) % 2 == 1
        held = jnp.where(
            upper,
            jnp.concatenate([taken, held], axis=0),
            jnp.concatenate([held, taken], axis=0),
        )
        size *= 2
    return held


def freq_pairs(groups, tiles):
    pairs = []
    for g in range(groups):
        for t in range(tiles):
            to = g + 1 if t % 2 == 0 else g - 1
            target = (to, t ^ 1) if 0 <= to < groups else (g, (t + 2) % tiles)
            pairs.append((g * tiles + t, target[0] * tiles + target[1]))
    return pairs


def body(sky_cube, kernel_one, bias_one, kernel_two, bias_two, kernel_three, bias_three):
    tiles, groups = lax.axis_size("tile"), lax.axis_size("freq")
    strip = sky_cube.shape[1] // tiles
    depth = tiles * sky_cube.shape[0]
    c1, c2, c3 = (kernel.shape[0] for kernel in (kernel_one, kernel_two, kernel_three))
    plan = Plan(strip, c1, c2, c3)

    w1 = jnp.transpose(kernel_one[:, 0], (1, 2, 3, 0))
    w2 = jnp.transpose(kernel_two, (2, 3, 4, 0, 1))
    w3 = jnp.transpose(kernel_three, (2, 3, 4, 1, 0))

    params = pltpu.CompilerParams(vmem_limit_bytes=32 * 2**20)
    bands_12 = pl.pallas_call(
        functools.partial(bands_12_kernel, plan),
        name="bands_12",
        out_shape=[
            jax.ShapeDtypeStruct((plan.r1 * c1, plan.k1), BF),
            jax.ShapeDtypeStruct((3, plan.r2 * c2, plan.k2), BF),
            jax.ShapeDtypeStruct((c1, 128), F32),
            jax.ShapeDtypeStruct((c2, 128), F32),
        ],
        in_specs=[SM] * 2 + [VM] * 2,
        out_specs=[VM] * 4,
        compiler_params=params,
    )(bias_one, bias_two, w1, w2)
    bands_3 = pl.pallas_call(
        functools.partial(bands_3_kernel, plan),
        name="bands_3",
        out_shape=[
            jax.ShapeDtypeStruct((3, plan.r3 * c3, plan.k3), BF),
            jax.ShapeDtypeStruct((plan.r3 * c3, 128), F32),
        ],
        in_specs=[SM, VM],
        out_specs=[VM] * 2,
        compiler_params=params,
    )(bias_three, w3)

    tile = lax.axis_index("tile")
    own = gathered(sky_cube, tiles)
    own, *bands_12 = lax.optimization_barrier((own, *bands_12))
    span = min(3 if tiles <= 4 else 4, tiles) * strip
    begin = (jnp.where(tile % 2 == 0, depth - 3, 0), first_row(plan, tile, tiles, span), 0)
    message = lax.dynamic_slice(own, begin, (3, span, own.shape[2]))
    got = lax.ppermute(message, ("freq", "tile"), freq_pairs(groups, tiles))
    got, *bands_3 = lax.optimization_barrier((got, *bands_3))
    other = lax.ppermute(got, "tile", [(t, t ^ 1) for t in range(tiles)])

    return pl.pallas_call(
        functools.partial(layers_kernel, plan, depth, span),
        name="layers",
        out_shape=jax.ShapeDtypeStruct((c3, depth // 2, plan.r3, sky_cube.shape[2] // 2), BF),
        in_specs=[VM] * 9,
        out_specs=VM,
        scratch_shapes=[
            pltpu.VMEM((plan.k2, (depth + 3) * 128), BF),
            pltpu.VMEM((plan.k3, (depth + 1) * 128), BF),
        ],
        compiler_params=params,
    )(own, got, other, *bands_12, *bands_3)


def solution(mesh):
    return jax.shard_map(
        body,
        mesh=mesh,
        in_specs=(P(("freq", "tile"), None, None), P(), P(), P(), P(), P(), P()),
        out_specs=P(None, "freq", "tile", None),
        check_vma=False,
    )
```

```python
import functools

import jax
import jax.numpy as jnp
from jax import lax
from jax.experimental import pallas as pl
from jax.experimental.pallas import tpu as pltpu
from jax.sharding import PartitionSpec as P

BF = jnp.bfloat16
F32 = jnp.float32
VM = pl.BlockSpec(memory_space=pltpu.VMEM)


def even(n):
    return n + n % 2


def up_to(n, unit):
    return -(-n // unit) * unit


class Plan:
    def __init__(self, strip, depth, c1, c2, c3):
        self.strip, self.depth, self.c1, self.c2, self.c3 = strip, depth, c1, c2, c3
        self.rim = 4
        self.slots = strip + 2 * self.rim
        self.span = 2 * strip + 2 * self.rim
        self.plane_k = up_to(3 * self.slots, 16)
        self.k1 = up_to(3 * self.plane_k, 256)
        self.block2, self.block3 = 6, 4
        self.r2 = up_to(strip + 1, self.block2)
        self.r1 = self.r2 + 2
        self.r3 = strip // 2
        self.n1, self.n2 = self.r1 * c1, self.r2 * c2
        self.in2, self.out2 = (self.block2 + 2) * c1, self.block2 * c2
        self.in3, self.out3 = (2 * self.block3 + 2) * c2, self.block3 * c3
        self.k2, self.k3 = up_to(3 * self.in2, 256), up_to(3 * self.in3, 256)
        self.planes1, self.planes2 = depth + 3, depth + 1


def leaky_relu(values):
    return jnp.maximum(values, 0.1 * values)


def faces_lower(tile):
    return tile % 2 == 1


def column_of(bias_ref, rows):
    at = lax.broadcasted_iota(jnp.int32, (rows, rows), 0)
    lane = lax.broadcasted_iota(jnp.int32, (rows, rows), 1)
    spread = jnp.where(at == lane, jnp.broadcast_to(bias_ref[...], (rows, rows)), 0.0)
    return jnp.broadcast_to(jnp.sum(spread, axis=1, keepdims=True), (rows, 128))


def ones_where(hit):
    return hit.astype(F32).astype(BF)


def dot_over_rows(left, right):
    return lax.dot_general(left, right, (((0,), (0,)), ((), ())), preferred_element_type=F32)


def rolled(x, by):
    return pltpu.roll(x, by, 1) if by else x


def bands_12_kernel(plan, bias1, bias2, bias3, w1, w2, t1, t2, b1, b2, b3):
    c1, c2 = plan.c1, plan.c2
    slots = plan.slots
    b1[...] = column_of(bias1, c1)
    b2[...] = column_of(bias2, c2)
    column = column_of(bias3, plan.c3)
    b3[...] = jnp.broadcast_to(column[:, None], b3.shape)
    tap = lax.broadcasted_iota(jnp.int32, (3, plan.k1), 0)
    lane = lax.broadcasted_iota(jnp.int32, (3, plan.k1), 1)
    taps = []
    for b in range(3):
        taps.append(
            sum(
                dot_over_rows(w1[a, b], ones_where(lane == a * plan.plane_k + tap * slots))
                for a in range(3)
            )
        )
    base = sum(rolled(taps[b], b) for b in range(3))
    for y in range(0, plan.r1, 2):
        rows = [rolled(base, y + k + plan.rim - 3) for k in range(2)]
        t1[y * c1 : (y + 2) * c1, :] = jnp.concatenate(rows, axis=0).astype(BF)

    for c in range(3):
        parts = [jnp.zeros((c2, 128), F32) for _ in range(plan.k2 // 128)]
        for a in range(3):
            for b in range(3):
                at = a * plan.in2 + b * c1
                tile = w2[a, b, c].astype(F32)
                tile = jnp.concatenate([tile, jnp.zeros((c2, 128 - c1), F32)], axis=1)
                parts[at // 128] += rolled(tile, at % 128)
        base = jnp.concatenate(parts, axis=1)
        for y in range(0, plan.block2, 2):
            rows = [rolled(base, (y + k) * c1) for k in range(2)]
            at = c * plan.out2 + y * c2
            t2[at : at + 2 * c2, :] = jnp.concatenate(rows, axis=0).astype(BF)


def bands_3_kernel(plan, w3, t3):
    c2, c3, rows = plan.c2, plan.c3, plan.block3
    n3 = plan.out3
    at = lax.broadcasted_iota(jnp.int32, (2 * n3, n3), 0)
    source = lax.broadcasted_iota(jnp.int32, (2 * n3, n3), 1)
    odd, pair, which, y = at // n3, (at % n3) // (2 * rows), (at // rows) % 2, at % rows
    turn = ones_where(source == y * c3 + 2 * pair + (which + odd) % 2)
    row = lax.broadcasted_iota(jnp.int32, (9 * c2, plan.k3), 0)
    lane = lax.broadcasted_iota(jnp.int32, (9 * c2, plan.k3), 1)
    a, b, i = row // (3 * c2), (row // c2) % 3, row % c2
    spread = ones_where(lane == a * plan.in3 + b * c2 + i)
    for c in range(3):
        taken = w3[:, :, c].astype(F32).reshape(9 * c2, c3).astype(BF)
        base = dot_over_rows(taken, spread)
        stacked = [rolled(base, 2 * y * c2) for y in range(rows)]
        stacked = jnp.concatenate(stacked, axis=0).astype(BF)
        both = jnp.dot(turn, stacked, preferred_element_type=F32).astype(BF)
        for odd in range(2):
            t3[odd, c * n3 : (c + 1) * n3, :] = both[odd * n3 : (odd + 1) * n3]


class Place:
    def __init__(self):
        freq, tile = lax.axis_index("freq"), lax.axis_index("tile")
        self.second = lax.rem(tile, 2) == 1
        self.faces_lower = faces_lower(tile)
        self.has_lower, self.has_upper = freq > 0, freq < lax.axis_size("freq") - 1
        self.has_above, self.has_below = tile > 0, tile < lax.axis_size("tile") - 1


def lane_of(x):
    return lax.broadcasted_iota(jnp.int32, x.shape, 1)


def turned(x, by):
    return pltpu.roll(x, by, 1)


def column_taps(x):
    lane, zero, half = lane_of(x), jnp.zeros_like(x), turned(x, 64)
    before = jnp.where(lane < 64, turned(x, 65), half)
    after = jnp.where(lane < 64, half, turned(x, 63))
    return jnp.where(lane == 0, zero, before), x, jnp.where(lane == 127, zero, after)


def sum_of_taps(before, here, after):
    lane, zero = lane_of(here), jnp.zeros_like(here)
    half = turned(jnp.where(lane < 64, before, after), 64)
    rest = jnp.where(lane < 64, turned(before, 65), turned(after, 63))
    return here + half + jnp.where((lane == 0) | (lane == 127), zero, rest)


def sum_of_even_taps(before, here, after):
    lane, zero = lane_of(here), jnp.zeros_like(here)
    return here + turned(after, 64) + jnp.where(lane == 0, zero, turned(before, 65))


def own_rows(own, plane):
    return own[plane].astype(F32)


def rim_rows(plan, place, ref, plane, inside):
    rows = ref[plane].astype(F32)
    rows = jnp.where(place.second, rows[plan.strip :], rows[: plan.slots])
    return jnp.where(inside, rows, 0.0)


def piece(plan, rows):
    pad = jnp.zeros((plan.plane_k - 3 * plan.slots, 128), F32)
    return jnp.concatenate([*column_taps(rows), pad], axis=0).astype(BF)


def in_twos(planes):
    planes = list(planes)
    return [planes[i : i + 2] for i in range(0, len(planes), 2)]


def layer_one(plan, place, pieces, planes, t1, b1):
    pad = jnp.zeros((plan.k1 - 3 * plan.plane_k, 128), BF)
    strip, made = plan.strip, {}
    for chunk in in_twos(planes):
        x1 = [jnp.concatenate([*pieces[p : p + 3], pad], axis=0) for p in chunk]
        sums = jnp.dot(t1[...], jnp.concatenate(x1, axis=1), preferred_element_type=F32)
        for i, p in enumerate(chunk):
            v = sums[:, i * 128 : (i + 1) * 128].reshape(plan.r1, plan.c1, 128)
            v = leaky_relu(v + b1[...])
            if p < 2:
                v = jnp.where(place.has_lower, v, 0.0)
            if p == plan.planes1 - 1:
                v = jnp.where(place.has_upper, v, 0.0)
            v = jnp.concatenate(
                [
                    jnp.where(place.has_above, v[:2], 0.0),
                    v[2 : strip + 2],
                    jnp.where(place.has_below, v[strip + 2 :], 0.0),
                ],
                axis=0,
            )
            made[p] = v.reshape(plan.n1, 128).astype(BF)
    return made


def blocks_of(planes, rows, step, size, k):
    parts = [plane[step * k : step * k + size] for plane in planes]
    return jnp.concatenate(parts + [jnp.zeros((rows - len(parts) * size, 128), BF)], axis=0)


def layer_two(plan, place, layer_one, planes, t2, b2):
    out2, blocks = plan.out2, {}
    for chunk in in_twos((q, k) for q in planes for k in range(plan.r2 // plan.block2)):
        x = []
        for q, k in chunk:
            x.append(blocks_of([layer_one(q + a) for a in range(3)], plan.k2, out2, plan.in2, k))
        sums = jnp.dot(t2[...], jnp.concatenate(x, axis=1), preferred_element_type=F32)
        for i, (q, k) in enumerate(chunk):
            taps = [sums[c * out2 : (c + 1) * out2, i * 128 : (i + 1) * 128] for c in range(3)]
            v = sum_of_taps(*taps).reshape(plan.block2, plan.c2, 128)
            v = leaky_relu(v + b2[...])
            if q == 0:
                v = jnp.where(place.has_lower, v, 0.0)
            if k == 0:
                v = jnp.concatenate([jnp.where(place.has_above, v[:1], 0.0), v[1:]], axis=0)
            blocks.setdefault(q, []).append(v.reshape(out2, 128).astype(BF))
    return {q: jnp.concatenate(parts, axis=0) for q, parts in blocks.items()}


def layer_three(plan, layer_two, t3, b3, out):
    n3, rows = plan.out3, plan.block3
    for chunk in in_twos(range(plan.depth // 2)):
        for y in range(0, plan.r3, 2 * rows):
            halves = []
            for odd in range(2):
                x = []
                for f in chunk:
                    planes = [layer_two(2 * f + a) for a in range(3)]
                    x.append(blocks_of(planes, plan.k3, 2 * rows * plan.c2, plan.in3, y // rows + odd))
                x = jnp.concatenate(x, axis=1)
                halves.append(jnp.dot(t3[odd], x, preferred_element_type=F32))
            for i, f in enumerate(chunk):
                first, second = (
                    sum_of_even_taps(
                        *(half[c * n3 : (c + 1) * n3, i * 128 : (i + 1) * 128] for c in range(3))
                    ).reshape(plan.c3 // 2, 2 * rows, 128)
                    for half in halves
                )
                sub = lax.broadcasted_iota(jnp.int32, first.shape, 1)
                one = jnp.where(sub < rows, first, second)
                other = jnp.where(sub < rows, second, first)
                other = jnp.concatenate([other[:, rows:], other[:, :rows]], axis=1)
                v = jnp.stack([one, other], axis=1).reshape(plan.c3, 2 * rows, 128)
                v = leaky_relu(v + b3[:, y : y + 2 * rows])
                out[:, f, y : y + 2 * rows] = v[:, :, :64].astype(BF)


def lower_half(plan, place, own, halo, middle, t1, t2, b1, b2):
    pieces = [piece(plan, rim_rows(plan, place, halo, p, place.has_lower)) for p in range(3)]
    pieces += [piece(plan, own_rows(own, p)) for p in range(2)]
    rim = layer_one(plan, place, pieces, range(3), t1, b1)
    return layer_two(plan, place, lambda p: rim[p] if p in rim else middle[p - 3], range(3), t2, b2)


def upper_half(plan, place, own, halo, middle, t1, t2, b1, b2):
    depth = plan.depth
    pieces = [None] * (depth + 1)
    pieces += [piece(plan, own_rows(own, p)) for p in (depth - 2, depth - 1)]
    pieces += [piece(plan, rim_rows(plan, place, halo, p, place.has_upper)) for p in range(2)]
    rim = layer_one(plan, place, pieces, range(depth + 1, depth + 3), t1, b1)
    some = lambda p: rim[p] if p in rim else middle[p - 3]
    return layer_two(plan, place, some, range(3, depth + 1), t2, b2)


def own_kernel(plan, own, t1, b1, middle):
    place, depth = Place(), plan.depth
    pieces = [None] * 3 + [piece(plan, own_rows(own, p)) for p in range(depth)]
    for p, v in layer_one(plan, place, pieces, range(3, depth + 1), t1, b1).items():
        middle[p - 3] = v


def early_kernel(plan, own, got, middle, t1, t2, b1, b2, done):
    place = Place()

    def run(half):
        for q, v in half(plan, place, own, got, middle, t1, t2, b1, b2).items():
            done[q] = v

    pl.when(place.faces_lower)(lambda: run(lower_half))
    pl.when(jnp.logical_not(place.faces_lower))(lambda: run(upper_half))


def late_kernel(plan, own, other, middle, done, t1, t2, b1, b2, t3, b3, out):
    place = Place()

    def run(half):
        late = half(plan, place, own, other, middle, t1, t2, b1, b2)
        layer_three(plan, lambda q: late[q] if q in late else done[q], t3, b3, out)

    pl.when(place.faces_lower)(lambda: run(upper_half))
    pl.when(jnp.logical_not(place.faces_lower))(lambda: run(lower_half))


def gathered(plane, tiles, beside):
    beside, ready = list(beside), []
    if tiles & (tiles - 1):
        return lax.all_gather(plane, "tile", axis=0, tiled=True), *sum(map(tuple, beside), ())
    tile, size, held = lax.axis_index("tile"), 1, plane
    while size < tiles:
        taken = lax.ppermute(held, "tile", [(t, t ^ (2 * size - 1)) for t in range(tiles)])
        if beside:
            taken, *made = lax.optimization_barrier((taken, *beside.pop(0)))
            ready += made
        upper = (tile // size) % 2 == 1
        held = jnp.where(
            upper,
            jnp.concatenate([taken, held], axis=0),
            jnp.concatenate([held, taken], axis=0),
        )
        size *= 2
    return held, *ready, *sum(map(tuple, beside), ())


def even_odd(cube):
    width = cube.shape[2]
    row = lax.broadcasted_iota(jnp.int32, (width, width), 0)
    col = lax.broadcasted_iota(jnp.int32, (width, width), 1)
    order = (row == 2 * (col % (width // 2)) + col // (width // 2)).astype(BF)
    return jnp.einsum("pyx,xw->pyw", cube.astype(BF), order, preferred_element_type=F32).astype(BF)


def freq_pairs(groups, tiles):
    pairs = []
    for g in range(groups):
        for t in range(tiles):
            to = g + 1 if t % 2 == 0 else g - 1
            target = (to, t ^ 1) if 0 <= to < groups else (g, (t + 2) % tiles)
            pairs.append((g * tiles + t, target[0] * tiles + target[1]))
    return pairs


def body(sky_cube, kernel_one, bias_one, kernel_two, bias_two, kernel_three, bias_three):
    tiles, groups = lax.axis_size("tile"), lax.axis_size("freq")
    strip = sky_cube.shape[1] // tiles
    depth = tiles * sky_cube.shape[0]
    c1, c2, c3 = (kernel.shape[0] for kernel in (kernel_one, kernel_two, kernel_three))
    plan = Plan(strip, depth, c1, c2, c3)
    tile = lax.axis_index("tile")

    w1 = jnp.transpose(kernel_one[:, 0], (1, 2, 3, 0))
    w2 = jnp.transpose(kernel_two, (2, 3, 4, 0, 1))
    w3 = jnp.transpose(kernel_three, (2, 3, 4, 1, 0))

    params = pltpu.CompilerParams(vmem_limit_bytes=32 * 2**20)
    bands_12 = pl.pallas_call(
        functools.partial(bands_12_kernel, plan),
        name="bands_12",
        out_shape=[
            jax.ShapeDtypeStruct((plan.n1, plan.k1), BF),
            jax.ShapeDtypeStruct((3 * plan.out2, plan.k2), BF),
            jax.ShapeDtypeStruct((c1, 128), F32),
            jax.ShapeDtypeStruct((c2, 128), F32),
            jax.ShapeDtypeStruct((c3, plan.r3, 128), F32),
        ],
        in_specs=[VM] * 5,
        out_specs=[VM] * 5,
        compiler_params=params,
    )(bias_one[None], bias_two[None], bias_three[None], w1, w2)
    planes = even_odd(sky_cube)
    own, t1, t2, b1, b2, b3 = gathered(planes, tiles, [(), bands_12])
    padded = jnp.pad(own, ((0, 0), (plan.rim, plan.rim), (0, 0)))
    width = own.shape[2]
    begin = (jnp.where(faces_lower(tile), 0, depth - 3), (tile // 2) * 2 * strip, 0)
    message = lax.dynamic_slice(padded, begin, (3, plan.span, width))
    message, w3 = lax.optimization_barrier((message, w3))
    got = lax.ppermute(message, ("freq", "tile"), freq_pairs(groups, tiles))
    own = lax.dynamic_slice(padded, (0, tile * strip, 0), (depth, plan.slots, width))
    bands_3 = pl.pallas_call(
        functools.partial(bands_3_kernel, plan),
        name="bands_3",
        out_shape=jax.ShapeDtypeStruct((2, 3 * plan.out3, plan.k3), BF),
        in_specs=[VM],
        out_specs=VM,
        compiler_params=params,
    )(w3)

    middle = pl.pallas_call(
        functools.partial(own_kernel, plan),
        name="own",
        out_shape=jax.ShapeDtypeStruct((depth - 2, plan.n1, 128), BF),
        in_specs=[VM] * 3,
        out_specs=VM,
        compiler_params=params,
    )(own, t1, b1)
    got, t3, middle = lax.optimization_barrier((got, bands_3, middle))
    other = lax.ppermute(got, "tile", [(t, t ^ 1) for t in range(tiles)])
    done = pl.pallas_call(
        functools.partial(early_kernel, plan),
        name="early",
        out_shape=jax.ShapeDtypeStruct((plan.planes2, plan.n2, 128), BF),
        in_specs=[VM] * 7,
        out_specs=VM,
        compiler_params=params,
    )(own, got, middle, t1, t2, b1, b2)
    other, done = lax.optimization_barrier((other, done))
    return pl.pallas_call(
        functools.partial(late_kernel, plan),
        name="late",
        out_shape=jax.ShapeDtypeStruct((c3, depth // 2, plan.r3, width // 2), BF),
        in_specs=[VM] * 10,
        out_specs=VM,
        compiler_params=params,
    )(own, other, middle, done, t1, t2, b1, b2, t3, b3)


def solution(mesh):
    return jax.shard_map(
        body,
        mesh=mesh,
        in_specs=(P(("freq", "tile"), None, None), P(), P(), P(), P(), P(), P()),
        out_specs=P(None, "freq", "tile", None),
        check_vma=False,
    )
```

```python
import functools

import jax
import jax.numpy as jnp
from jax import lax
from jax.experimental import pallas as pl
from jax.experimental.pallas import tpu as pltpu
from jax.sharding import PartitionSpec as P

BF = jnp.bfloat16
F32 = jnp.float32
VM = pl.BlockSpec(memory_space=pltpu.VMEM)


def even(n):
    return n + n % 2


def up_to(n, unit):
    return -(-n // unit) * unit


class Plan:
    def __init__(self, strip, depth, c1, c2, c3):
        self.strip, self.depth, self.c1, self.c2, self.c3 = strip, depth, c1, c2, c3
        self.rim = 4
        self.slots = strip + 2 * self.rim
        self.span = 2 * strip + 2 * self.rim
        self.plane_k = up_to(3 * self.slots, 16)
        self.k1 = up_to(3 * self.plane_k, 256)
        self.block2, self.block3 = 6, 4
        self.r2 = up_to(strip + 1, self.block2)
        self.r1 = self.r2 + 2
        self.r3 = strip // 2
        self.n1, self.n2 = self.r1 * c1, self.r2 * c2
        self.in2, self.out2 = (self.block2 + 2) * c1, self.block2 * c2
        self.in3, self.out3 = (2 * self.block3 + 2) * c2, self.block3 * c3
        self.k2, self.k3 = up_to(3 * self.in2, 256), up_to(3 * self.in3, 256)
        self.planes1, self.planes2 = depth + 3, depth + 1


def leaky_relu(values):
    return jnp.maximum(values, 0.1 * values)


def faces_lower(tile):
    return tile % 2 == 1


def column_of(bias_ref, rows):
    at = lax.broadcasted_iota(jnp.int32, (rows, rows), 0)
    lane = lax.broadcasted_iota(jnp.int32, (rows, rows), 1)
    spread = jnp.where(at == lane, jnp.broadcast_to(bias_ref[...], (rows, rows)), 0.0)
    return jnp.broadcast_to(jnp.sum(spread, axis=1, keepdims=True), (rows, 128))


def ones_where(hit):
    return hit.astype(F32).astype(BF)


def dot_over_rows(left, right):
    return lax.dot_general(left, right, (((0,), (0,)), ((), ())), preferred_element_type=F32)


def rolled(x, by):
    return pltpu.roll(x, by, 1) if by else x


def bands_12_kernel(plan, bias1, bias2, bias3, w1, w2, t1, t2, b1, b2, b3):
    c1, c2 = plan.c1, plan.c2
    slots = plan.slots
    b1[...] = column_of(bias1, c1)
    b2[...] = column_of(bias2, c2)
    column = column_of(bias3, plan.c3)
    b3[...] = jnp.broadcast_to(column[:, None], b3.shape)
    tap = lax.broadcasted_iota(jnp.int32, (3, plan.k1), 0)
    lane = lax.broadcasted_iota(jnp.int32, (3, plan.k1), 1)
    taps = []
    for b in range(3):
        taps.append(
            sum(
                dot_over_rows(w1[a, b], ones_where(lane == a * plan.plane_k + tap * slots))
                for a in range(3)
            )
        )
    base = sum(rolled(taps[b], b) for b in range(3))
    for y in range(0, plan.r1, 2):
        rows = [rolled(base, y + k + plan.rim - 3) for k in range(2)]
        t1[y * c1 : (y + 2) * c1, :] = jnp.concatenate(rows, axis=0).astype(BF)

    for c in range(3):
        parts = [jnp.zeros((c2, 128), F32) for _ in range(plan.k2 // 128)]
        for a in range(3):
            for b in range(3):
                at = a * plan.in2 + b * c1
                tile = w2[a, b, c].astype(F32)
                tile = jnp.concatenate([tile, jnp.zeros((c2, 128 - c1), F32)], axis=1)
                parts[at // 128] += rolled(tile, at % 128)
        base = jnp.concatenate(parts, axis=1)
        for y in range(0, plan.block2, 2):
            rows = [rolled(base, (y + k) * c1) for k in range(2)]
            at = c * plan.out2 + y * c2
            t2[at : at + 2 * c2, :] = jnp.concatenate(rows, axis=0).astype(BF)


def bands_3_kernel(plan, w3, t3):
    c2, c3, rows = plan.c2, plan.c3, plan.block3
    n3 = plan.out3
    at = lax.broadcasted_iota(jnp.int32, (2 * n3, n3), 0)
    source = lax.broadcasted_iota(jnp.int32, (2 * n3, n3), 1)
    odd, pair, which, y = at // n3, (at % n3) // (2 * rows), (at // rows) % 2, at % rows
    turn = ones_where(source == y * c3 + 2 * pair + (which + odd) % 2)
    row = lax.broadcasted_iota(jnp.int32, (9 * c2, plan.k3), 0)
    lane = lax.broadcasted_iota(jnp.int32, (9 * c2, plan.k3), 1)
    a, b, i = row // (3 * c2), (row // c2) % 3, row % c2
    spread = ones_where(lane == a * plan.in3 + b * c2 + i)
    for c in range(3):
        taken = w3[:, :, c].astype(F32).reshape(9 * c2, c3).astype(BF)
        base = dot_over_rows(taken, spread)
        stacked = [rolled(base, 2 * y * c2) for y in range(rows)]
        stacked = jnp.concatenate(stacked, axis=0).astype(BF)
        both = jnp.dot(turn, stacked, preferred_element_type=F32).astype(BF)
        for odd in range(2):
            t3[odd, c * n3 : (c + 1) * n3, :] = both[odd * n3 : (odd + 1) * n3]


class Place:
    def __init__(self):
        freq, tile = lax.axis_index("freq"), lax.axis_index("tile")
        self.second = lax.rem(tile, 2) == 1
        self.faces_lower = faces_lower(tile)
        self.has_lower, self.has_upper = freq > 0, freq < lax.axis_size("freq") - 1
        self.has_above, self.has_below = tile > 0, tile < lax.axis_size("tile") - 1


def lane_of(x):
    return lax.broadcasted_iota(jnp.int32, x.shape, 1)


def turned(x, by):
    return pltpu.roll(x, by, 1)


def column_taps(x):
    lane, zero, half = lane_of(x), jnp.zeros_like(x), turned(x, 64)
    before = jnp.where(lane < 64, turned(x, 65), half)
    after = jnp.where(lane < 64, half, turned(x, 63))
    return jnp.where(lane == 0, zero, before), x, jnp.where(lane == 127, zero, after)


def sum_of_taps(before, here, after):
    lane, zero = lane_of(here), jnp.zeros_like(here)
    half = turned(jnp.where(lane < 64, before, after), 64)
    rest = jnp.where(lane < 64, turned(before, 65), turned(after, 63))
    return here + half + jnp.where((lane == 0) | (lane == 127), zero, rest)


def sum_of_even_taps(before, here, after):
    lane, zero = lane_of(here), jnp.zeros_like(here)
    return here + turned(after, 64) + jnp.where(lane == 0, zero, turned(before, 65))


def own_rows(plan, place, ref, plane):
    rows = ref[plane].astype(F32)
    return jnp.where(place.second, rows[plan.strip :], rows[: plan.slots])


def rim_rows(plan, place, ref, plane, inside):
    return jnp.where(inside, own_rows(plan, place, ref, plane), 0.0)


def piece(plan, rows):
    pad = jnp.zeros((plan.plane_k - 3 * plan.slots, 128), F32)
    return jnp.concatenate([*column_taps(rows), pad], axis=0).astype(BF)


def in_twos(planes):
    planes = list(planes)
    return [planes[i : i + 2] for i in range(0, len(planes), 2)]


def layer_one(plan, place, pieces, planes, t1, b1):
    pad = jnp.zeros((plan.k1 - 3 * plan.plane_k, 128), BF)
    strip, made = plan.strip, {}
    for chunk in in_twos(planes):
        x1 = [jnp.concatenate([*pieces[p : p + 3], pad], axis=0) for p in chunk]
        sums = jnp.dot(t1[...], jnp.concatenate(x1, axis=1), preferred_element_type=F32)
        for i, p in enumerate(chunk):
            v = sums[:, i * 128 : (i + 1) * 128].reshape(plan.r1, plan.c1, 128)
            v = leaky_relu(v + b1[...])
            if p < 2:
                v = jnp.where(place.has_lower, v, 0.0)
            if p == plan.planes1 - 1:
                v = jnp.where(place.has_upper, v, 0.0)
            v = jnp.concatenate(
                [
                    jnp.where(place.has_above, v[:2], 0.0),
                    v[2 : strip + 2],
                    jnp.where(place.has_below, v[strip + 2 :], 0.0),
                ],
                axis=0,
            )
            made[p] = v.reshape(plan.n1, 128).astype(BF)
    return made


def blocks_of(planes, rows, step, size, k):
    parts = [plane[step * k : step * k + size] for plane in planes]
    return jnp.concatenate(parts + [jnp.zeros((rows - len(parts) * size, 128), BF)], axis=0)


def layer_two(plan, place, layer_one, planes, t2, b2):
    out2, blocks = plan.out2, {}
    for chunk in in_twos((q, k) for q in planes for k in range(plan.r2 // plan.block2)):
        x = []
        for q, k in chunk:
            x.append(blocks_of([layer_one(q + a) for a in range(3)], plan.k2, out2, plan.in2, k))
        sums = jnp.dot(t2[...], jnp.concatenate(x, axis=1), preferred_element_type=F32)
        for i, (q, k) in enumerate(chunk):
            taps = [sums[c * out2 : (c + 1) * out2, i * 128 : (i + 1) * 128] for c in range(3)]
            v = sum_of_taps(*taps).reshape(plan.block2, plan.c2, 128)
            v = leaky_relu(v + b2[...])
            if q == 0:
                v = jnp.where(place.has_lower, v, 0.0)
            if k == 0:
                v = jnp.concatenate([jnp.where(place.has_above, v[:1], 0.0), v[1:]], axis=0)
            blocks.setdefault(q, []).append(v.reshape(out2, 128).astype(BF))
    return {q: jnp.concatenate(parts, axis=0) for q, parts in blocks.items()}


def layer_three(plan, layer_two, t3, b3, out):
    n3, rows = plan.out3, plan.block3
    for chunk in in_twos(range(plan.depth // 2)):
        for y in range(0, plan.r3, 2 * rows):
            halves = []
            for odd in range(2):
                x = []
                for f in chunk:
                    planes = [layer_two(2 * f + a) for a in range(3)]
                    x.append(blocks_of(planes, plan.k3, 2 * rows * plan.c2, plan.in3, y // rows + odd))
                x = jnp.concatenate(x, axis=1)
                halves.append(jnp.dot(t3[odd], x, preferred_element_type=F32))
            for i, f in enumerate(chunk):
                first, second = (
                    sum_of_even_taps(
                        *(half[c * n3 : (c + 1) * n3, i * 128 : (i + 1) * 128] for c in range(3))
                    ).reshape(plan.c3 // 2, 2 * rows, 128)
                    for half in halves
                )
                sub = lax.broadcasted_iota(jnp.int32, first.shape, 1)
                one = jnp.where(sub < rows, first, second)
                other = jnp.where(sub < rows, second, first)
                other = jnp.concatenate([other[:, rows:], other[:, :rows]], axis=1)
                v = jnp.stack([one, other], axis=1).reshape(plan.c3, 2 * rows, 128)
                v = leaky_relu(v + b3[:, y : y + 2 * rows])
                out[:, f, y : y + 2 * rows] = v[:, :, :64].astype(BF)


def lower_half(plan, place, own, halo, middle, t1, t2, b1, b2):
    pieces = [piece(plan, rim_rows(plan, place, halo, p, place.has_lower)) for p in range(3)]
    pieces += [piece(plan, own_rows(plan, place, own, p)) for p in range(2)]
    rim = layer_one(plan, place, pieces, range(3), t1, b1)
    return layer_two(plan, place, lambda p: rim[p] if p in rim else middle[p - 3], range(3), t2, b2)


def upper_half(plan, place, own, halo, middle, t1, t2, b1, b2):
    depth = plan.depth
    pieces = [None] * (depth + 1)
    pieces += [piece(plan, own_rows(plan, place, own, p)) for p in (depth - 2, depth - 1)]
    pieces += [piece(plan, rim_rows(plan, place, halo, p, place.has_upper)) for p in range(2)]
    rim = layer_one(plan, place, pieces, range(depth + 1, depth + 3), t1, b1)
    some = lambda p: rim[p] if p in rim else middle[p - 3]
    return layer_two(plan, place, some, range(3, depth + 1), t2, b2)


def own_kernel(plan, own, t1, b1, middle):
    place, depth = Place(), plan.depth
    pieces = [None] * 3 + [piece(plan, own_rows(plan, place, own, p)) for p in range(depth)]
    for p, v in layer_one(plan, place, pieces, range(3, depth + 1), t1, b1).items():
        middle[p - 3] = v


def early_kernel(plan, own, got, middle, t1, t2, b1, b2, done):
    place = Place()

    def run(half):
        for q, v in half(plan, place, own, got, middle, t1, t2, b1, b2).items():
            done[q] = v

    pl.when(place.faces_lower)(lambda: run(lower_half))
    pl.when(jnp.logical_not(place.faces_lower))(lambda: run(upper_half))


def late_kernel(plan, own, other, middle, done, t1, t2, b1, b2, t3, b3, out):
    place = Place()

    def run(half):
        late = half(plan, place, own, other, middle, t1, t2, b1, b2)
        layer_three(plan, lambda q: late[q] if q in late else done[q], t3, b3, out)

    pl.when(place.faces_lower)(lambda: run(upper_half))
    pl.when(jnp.logical_not(place.faces_lower))(lambda: run(lower_half))


def in_order(upper, held, taken):
    return jnp.where(
        upper,
        jnp.concatenate([taken, held], axis=0),
        jnp.concatenate([held, taken], axis=0),
    )


def chip_rows(plan, planes, chip):
    padded = jnp.pad(planes, ((0, 0), (plan.rim, plan.rim), (0, 0)))
    shape = (planes.shape[0], plan.span, planes.shape[2])
    return lax.dynamic_slice(padded, (0, chip * 2 * plan.strip, 0), shape)


def freq_pairs(groups, tiles, flip):
    pairs = []
    for g in range(groups):
        for t in range(tiles):
            to = g + 1 if t % 2 == 0 else g - 1
            target = (to, t ^ flip) if 0 <= to < groups else (g, (t + 2) % tiles)
            pairs.append((g * tiles + t, target[0] * tiles + target[1]))
    return pairs


def gathered(plan, plane, tiles):
    if tiles & (tiles - 1):
        held = lax.all_gather(plane, "tile", axis=0, tiled=True)
        return chip_rows(plan, held, lax.axis_index("tile") // 2)
    tile, size, held = lax.axis_index("tile"), 1, plane
    while size < tiles:
        taken = lax.ppermute(held, "tile", [(t, t ^ (2 * size - 1)) for t in range(tiles)])
        held = in_order((tile // size) % 2 == 1, held, taken)
        size *= 2
    return chip_rows(plan, held, tile // 2)


def some_planes(planes, tile):
    begin = (jnp.where(faces_lower(tile), planes.shape[0] - 3, 0), 0, 0)
    return lax.dynamic_slice(planes, begin, (3, *planes.shape[1:]))


def exchanged(plan, plane, groups, tiles, weights):
    axes, tile = ("freq", "tile"), lax.axis_index("tile")
    if tiles != 4:
        own = gathered(plan, plane, tiles)
        message = some_planes(own, tile + 1)
        return own, lax.ppermute(message, axes, freq_pairs(groups, tiles, 1)), weights
    taken = lax.ppermute(plane, "tile", [(t, t ^ 1) for t in range(tiles)])
    pair = in_order(tile % 2 == 1, plane, taken)
    chip = tile // 2
    mine, theirs = chip_rows(plan, pair, chip), chip_rows(plan, pair, 1 - chip)
    across = lax.ppermute(theirs, "tile", [(t, t ^ 3) for t in range(tiles)])
    ahead = lax.ppermute(mine, axes, freq_pairs(groups, tiles, 1))
    aside = lax.ppermute(theirs, axes, freq_pairs(groups, tiles, 3))
    across, *weights = lax.optimization_barrier((across, *weights))
    own = in_order(chip == 1, mine, across)
    return own, some_planes(in_order(chip == 1, ahead, aside), tile), weights


def even_odd(cube):
    width = cube.shape[2]
    row = lax.broadcasted_iota(jnp.int32, (width, width), 0)
    col = lax.broadcasted_iota(jnp.int32, (width, width), 1)
    order = (row == 2 * (col % (width // 2)) + col // (width // 2)).astype(BF)
    return jnp.einsum("pyx,xw->pyw", cube.astype(BF), order, preferred_element_type=F32).astype(BF)


def body(sky_cube, kernel_one, bias_one, kernel_two, bias_two, kernel_three, bias_three):
    tiles, groups = lax.axis_size("tile"), lax.axis_size("freq")
    strip = sky_cube.shape[1] // tiles
    depth = tiles * sky_cube.shape[0]
    c1, c2, c3 = (kernel.shape[0] for kernel in (kernel_one, kernel_two, kernel_three))
    plan = Plan(strip, depth, c1, c2, c3)
    tile = lax.axis_index("tile")

    w1 = jnp.transpose(kernel_one[:, 0], (1, 2, 3, 0))
    w2 = jnp.transpose(kernel_two, (2, 3, 4, 0, 1))
    w3 = jnp.transpose(kernel_three, (2, 3, 4, 1, 0))

    own, got, weights = exchanged(
        plan, even_odd(sky_cube), groups, tiles, (bias_one[None], bias_two[None], bias_three[None], w1, w2, w3)
    )
    bias_one, bias_two, bias_three, w1, w2, w3 = weights
    params = pltpu.CompilerParams(vmem_limit_bytes=32 * 2**20)
    bands_12 = pl.pallas_call(
        functools.partial(bands_12_kernel, plan),
        name="bands_12",
        out_shape=[
            jax.ShapeDtypeStruct((plan.n1, plan.k1), BF),
            jax.ShapeDtypeStruct((3 * plan.out2, plan.k2), BF),
            jax.ShapeDtypeStruct((c1, 128), F32),
            jax.ShapeDtypeStruct((c2, 128), F32),
            jax.ShapeDtypeStruct((c3, plan.r3, 128), F32),
        ],
        in_specs=[VM] * 5,
        out_specs=[VM] * 5,
        compiler_params=params,
    )(bias_one, bias_two, bias_three, w1, w2)
    bands_3 = pl.pallas_call(
        functools.partial(bands_3_kernel, plan),
        name="bands_3",
        out_shape=jax.ShapeDtypeStruct((2, 3 * plan.out3, plan.k3), BF),
        in_specs=[VM],
        out_specs=VM,
        compiler_params=params,
    )(w3)

    t1, t2, b1, b2, b3 = bands_12
    middle = pl.pallas_call(
        functools.partial(own_kernel, plan),
        name="own",
        out_shape=jax.ShapeDtypeStruct((depth - 2, plan.n1, 128), BF),
        in_specs=[VM] * 3,
        out_specs=VM,
        compiler_params=params,
    )(own, t1, b1)
    got, t3, middle = lax.optimization_barrier((got, bands_3, middle))
    other = lax.ppermute(got, "tile", [(t, t ^ 1) for t in range(tiles)])
    done = pl.pallas_call(
        functools.partial(early_kernel, plan),
        name="early",
        out_shape=jax.ShapeDtypeStruct((plan.planes2, plan.n2, 128), BF),
        in_specs=[VM] * 7,
        out_specs=VM,
        compiler_params=params,
    )(own, got, middle, t1, t2, b1, b2)
    other, done = lax.optimization_barrier((other, done))
    return pl.pallas_call(
        functools.partial(late_kernel, plan),
        name="late",
        out_shape=jax.ShapeDtypeStruct((c3, depth // 2, plan.r3, sky_cube.shape[2] // 2), BF),
        in_specs=[VM] * 10,
        out_specs=VM,
        compiler_params=params,
    )(own, other, middle, done, t1, t2, b1, b2, t3, b3)


def solution(mesh):
    return jax.shard_map(
        body,
        mesh=mesh,
        in_specs=(P(("freq", "tile"), None, None), P(), P(), P(), P(), P(), P()),
        out_specs=P(None, "freq", "tile", None),
        check_vma=False,
    )
```

```python
import functools

import jax
import jax.numpy as jnp
from jax import lax
from jax.experimental import pallas as pl
from jax.experimental.pallas import tpu as pltpu
from jax.sharding import PartitionSpec as P

BF = jnp.bfloat16
F32 = jnp.float32
VM = pl.BlockSpec(memory_space=pltpu.VMEM)


def even(n):
    return n + n % 2


def up_to(n, unit):
    return -(-n // unit) * unit


class Plan:
    def __init__(self, strip, depth, c1, c2, c3):
        self.strip, self.depth, self.c1, self.c2, self.c3 = strip, depth, c1, c2, c3
        self.rim = 4
        self.slots = strip + 2 * self.rim
        self.span = 2 * strip + 2 * self.rim
        self.plane_k = up_to(3 * self.slots, 16)
        self.k1 = up_to(3 * self.plane_k, 256)
        self.block2, self.block3 = 6, 4
        self.r2 = up_to(strip + 1, self.block2)
        self.r1 = self.r2 + 2
        self.r3 = strip // 2
        self.n1, self.n2 = self.r1 * c1, self.r2 * c2
        self.in2, self.out2 = (self.block2 + 2) * c1, self.block2 * c2
        self.in3, self.out3 = (2 * self.block3 + 2) * c2, self.block3 * c3
        self.k2, self.k3 = up_to(3 * self.in2, 256), up_to(3 * self.in3, 256)
        self.planes1, self.planes2 = depth + 3, depth + 1


def leaky_relu(values):
    return jnp.maximum(values, 0.1 * values)


def faces_lower(tile):
    return tile % 2 == 1


def column_of(bias_ref, rows):
    at = lax.broadcasted_iota(jnp.int32, (rows, rows), 0)
    lane = lax.broadcasted_iota(jnp.int32, (rows, rows), 1)
    spread = jnp.where(at == lane, jnp.broadcast_to(bias_ref[...], (rows, rows)), 0.0)
    return jnp.broadcast_to(jnp.sum(spread, axis=1, keepdims=True), (rows, 128))


def ones_where(hit):
    return hit.astype(F32).astype(BF)


def dot_over_rows(left, right):
    return lax.dot_general(left, right, (((0,), (0,)), ((), ())), preferred_element_type=F32)


def rolled(x, by):
    return pltpu.roll(x, by, 1) if by else x


def bands_12_kernel(plan, bias1, bias2, bias3, w1, w2, t1, t2, b1, b2, b3):
    c1, c2 = plan.c1, plan.c2
    slots = plan.slots
    b1[...] = column_of(bias1, c1)
    b2[...] = column_of(bias2, c2)
    column = column_of(bias3, plan.c3)
    b3[...] = jnp.broadcast_to(column[:, None], b3.shape)
    tap = lax.broadcasted_iota(jnp.int32, (3, plan.k1), 0)
    lane = lax.broadcasted_iota(jnp.int32, (3, plan.k1), 1)
    taps = []
    for b in range(3):
        taps.append(
            sum(
                dot_over_rows(w1[a, b], ones_where(lane == a * plan.plane_k + tap * slots))
                for a in range(3)
            )
        )
    base = sum(rolled(taps[b], b) for b in range(3))
    for y in range(0, plan.r1, 2):
        rows = [rolled(base, y + k + plan.rim - 3) for k in range(2)]
        t1[y * c1 : (y + 2) * c1, :] = jnp.concatenate(rows, axis=0).astype(BF)

    for c in range(3):
        parts = [jnp.zeros((c2, 128), F32) for _ in range(plan.k2 // 128)]
        for a in range(3):
            for b in range(3):
                at = a * plan.in2 + b * c1
                tile = w2[a, b, c].astype(F32)
                tile = jnp.concatenate([tile, jnp.zeros((c2, 128 - c1), F32)], axis=1)
                parts[at // 128] += rolled(tile, at % 128)
        base = jnp.concatenate(parts, axis=1)
        for y in range(0, plan.block2, 2):
            rows = [rolled(base, (y + k) * c1) for k in range(2)]
            at = c * plan.out2 + y * c2
            t2[at : at + 2 * c2, :] = jnp.concatenate(rows, axis=0).astype(BF)


def bands_3_kernel(plan, w3, t3):
    c2, c3, rows = plan.c2, plan.c3, plan.block3
    n3 = plan.out3
    at = lax.broadcasted_iota(jnp.int32, (2 * n3, n3), 0)
    source = lax.broadcasted_iota(jnp.int32, (2 * n3, n3), 1)
    odd, pair, which, y = at // n3, (at % n3) // (2 * rows), (at // rows) % 2, at % rows
    turn = ones_where(source == y * c3 + 2 * pair + (which + odd) % 2)
    row = lax.broadcasted_iota(jnp.int32, (9 * c2, plan.k3), 0)
    lane = lax.broadcasted_iota(jnp.int32, (9 * c2, plan.k3), 1)
    a, b, i = row // (3 * c2), (row // c2) % 3, row % c2
    spread = ones_where(lane == a * plan.in3 + b * c2 + i)
    for c in range(3):
        taken = w3[:, :, c].astype(F32).reshape(9 * c2, c3).astype(BF)
        base = dot_over_rows(taken, spread)
        stacked = [rolled(base, 2 * y * c2) for y in range(rows)]
        stacked = jnp.concatenate(stacked, axis=0).astype(BF)
        both = jnp.dot(turn, stacked, preferred_element_type=F32).astype(BF)
        for odd in range(2):
            t3[odd, c * n3 : (c + 1) * n3, :] = both[odd * n3 : (odd + 1) * n3]


class Place:
    def __init__(self):
        freq, tile = lax.axis_index("freq"), lax.axis_index("tile")
        self.second = lax.rem(tile, 2) == 1
        self.faces_lower = faces_lower(tile)
        self.has_lower, self.has_upper = freq > 0, freq < lax.axis_size("freq") - 1
        self.has_above, self.has_below = tile > 0, tile < lax.axis_size("tile") - 1


def lane_of(x):
    return lax.broadcasted_iota(jnp.int32, x.shape, 1)


def turned(x, by):
    return pltpu.roll(x, by, 1)


def column_taps(x):
    lane, zero, half = lane_of(x), jnp.zeros_like(x), turned(x, 64)
    before = jnp.where(lane < 64, turned(x, 65), half)
    after = jnp.where(lane < 64, half, turned(x, 63))
    return jnp.where(lane == 0, zero, before), x, jnp.where(lane == 127, zero, after)


def sum_of_taps(before, here, after):
    lane, zero = lane_of(here), jnp.zeros_like(here)
    half = turned(jnp.where(lane < 64, before, after), 64)
    rest = jnp.where(lane < 64, turned(before, 65), turned(after, 63))
    return here + half + jnp.where((lane == 0) | (lane == 127), zero, rest)


def sum_of_even_taps(before, here, after):
    lane, zero = lane_of(here), jnp.zeros_like(here)
    return here + turned(after, 64) + jnp.where(lane == 0, zero, turned(before, 65))


def own_rows(plan, place, ref, plane):
    rows = ref[plane].astype(F32)
    return jnp.where(place.second, rows[plan.strip :], rows[: plan.slots])


def rim_rows(plan, place, ref, plane, inside):
    return jnp.where(inside, own_rows(plan, place, ref, plane), 0.0)


def piece(plan, rows):
    pad = jnp.zeros((plan.plane_k - 3 * plan.slots, 128), F32)
    return jnp.concatenate([*column_taps(rows), pad], axis=0).astype(BF)


def in_twos(planes):
    planes = list(planes)
    return [planes[i : i + 2] for i in range(0, len(planes), 2)]


def layer_one(plan, place, pieces, planes, t1, b1):
    pad = jnp.zeros((plan.k1 - 3 * plan.plane_k, 128), BF)
    strip, made = plan.strip, {}
    for chunk in in_twos(planes):
        x1 = [jnp.concatenate([*pieces[p : p + 3], pad], axis=0) for p in chunk]
        sums = jnp.dot(t1[...], jnp.concatenate(x1, axis=1), preferred_element_type=F32)
        for i, p in enumerate(chunk):
            v = sums[:, i * 128 : (i + 1) * 128].reshape(plan.r1, plan.c1, 128)
            v = leaky_relu(v + b1[...])
            if p < 2:
                v = jnp.where(place.has_lower, v, 0.0)
            if p == plan.planes1 - 1:
                v = jnp.where(place.has_upper, v, 0.0)
            v = jnp.concatenate(
                [
                    jnp.where(place.has_above, v[:2], 0.0),
                    v[2 : strip + 2],
                    jnp.where(place.has_below, v[strip + 2 :], 0.0),
                ],
                axis=0,
            )
            made[p] = v.reshape(plan.n1, 128).astype(BF)
    return made


def blocks_of(planes, rows, step, size, k):
    parts = [plane[step * k : step * k + size] for plane in planes]
    return jnp.concatenate(parts + [jnp.zeros((rows - len(parts) * size, 128), BF)], axis=0)


def layer_two(plan, place, layer_one, planes, t2, b2):
    out2, blocks = plan.out2, {}
    for chunk in in_twos((q, k) for q in planes for k in range(plan.r2 // plan.block2)):
        x = []
        for q, k in chunk:
            x.append(blocks_of([layer_one(q + a) for a in range(3)], plan.k2, out2, plan.in2, k))
        sums = jnp.dot(t2[...], jnp.concatenate(x, axis=1), preferred_element_type=F32)
        for i, (q, k) in enumerate(chunk):
            taps = [sums[c * out2 : (c + 1) * out2, i * 128 : (i + 1) * 128] for c in range(3)]
            v = sum_of_taps(*taps).reshape(plan.block2, plan.c2, 128)
            v = leaky_relu(v + b2[...])
            if q == 0:
                v = jnp.where(place.has_lower, v, 0.0)
            if k == 0:
                v = jnp.concatenate([jnp.where(place.has_above, v[:1], 0.0), v[1:]], axis=0)
            blocks.setdefault(q, []).append(v.reshape(out2, 128).astype(BF))
    return {q: jnp.concatenate(parts, axis=0) for q, parts in blocks.items()}


def layer_three(plan, layer_two, t3, b3, out):
    n3, rows = plan.out3, plan.block3
    for chunk in in_twos(range(plan.depth // 2)):
        for y in range(0, plan.r3, 2 * rows):
            halves = []
            for odd in range(2):
                x = []
                for f in chunk:
                    planes = [layer_two(2 * f + a) for a in range(3)]
                    x.append(blocks_of(planes, plan.k3, 2 * rows * plan.c2, plan.in3, y // rows + odd))
                x = jnp.concatenate(x, axis=1)
                halves.append(jnp.dot(t3[odd], x, preferred_element_type=F32))
            for i, f in enumerate(chunk):
                first, second = (
                    sum_of_even_taps(
                        *(half[c * n3 : (c + 1) * n3, i * 128 : (i + 1) * 128] for c in range(3))
                    ).reshape(plan.c3 // 2, 2 * rows, 128)
                    for half in halves
                )
                sub = lax.broadcasted_iota(jnp.int32, first.shape, 1)
                one = jnp.where(sub < rows, first, second)
                other = jnp.where(sub < rows, second, first)
                other = jnp.concatenate([other[:, rows:], other[:, :rows]], axis=1)
                v = jnp.stack([one, other], axis=1).reshape(plan.c3, 2 * rows, 128)
                v = leaky_relu(v + b3[:, y : y + 2 * rows])
                out[:, f, y : y + 2 * rows] = v[:, :, :64].astype(BF)


def lower_half(plan, place, own, halo, t1, t2, b1, b2, middle=None):
    pieces = [piece(plan, rim_rows(plan, place, halo, p, place.has_lower)) for p in range(3)]
    pieces += [piece(plan, own_rows(plan, place, own, p)) for p in range(plan.depth if middle is None else 2)]
    made = layer_one(plan, place, pieces, range(plan.depth + 1 if middle is None else 3), t1, b1)
    some = lambda p: made[p] if p in made else middle[p - 3]
    return layer_two(plan, place, some, range(3), t2, b2), made


def upper_half(plan, place, own, halo, t1, t2, b1, b2, middle=None):
    depth = plan.depth
    first = 0 if middle is None else depth - 2
    pieces = [None] * (3 + first)
    pieces += [piece(plan, own_rows(plan, place, own, p)) for p in range(first, depth)]
    pieces += [piece(plan, rim_rows(plan, place, halo, p, place.has_upper)) for p in range(2)]
    made = layer_one(plan, place, pieces, range(3 + first, depth + 3), t1, b1)
    some = lambda p: made[p] if p in made else middle[p - 3]
    return layer_two(plan, place, some, range(3, depth + 1), t2, b2), made


def early_kernel(plan, own, got, t1, t2, b1, b2, done, middle):
    place = Place()

    def run(half):
        planes, made = half(plan, place, own, got, t1, t2, b1, b2)
        for q, v in planes.items():
            done[q] = v
        for p in range(3, plan.depth + 1):
            middle[p - 3] = made[p]

    pl.when(place.faces_lower)(lambda: run(lower_half))
    pl.when(jnp.logical_not(place.faces_lower))(lambda: run(upper_half))


def late_kernel(plan, own, other, middle, done, t1, t2, b1, b2, t3, b3, out):
    place = Place()

    def run(half):
        late, _ = half(plan, place, own, other, t1, t2, b1, b2, middle)
        layer_three(plan, lambda q: late[q] if q in late else done[q], t3, b3, out)

    pl.when(place.faces_lower)(lambda: run(upper_half))
    pl.when(jnp.logical_not(place.faces_lower))(lambda: run(lower_half))


def in_order(upper, held, taken):
    return jnp.where(
        upper,
        jnp.concatenate([taken, held], axis=0),
        jnp.concatenate([held, taken], axis=0),
    )


def chip_rows(plan, planes, chip):
    padded = jnp.pad(planes, ((0, 0), (plan.rim, plan.rim), (0, 0)))
    shape = (planes.shape[0], plan.span, planes.shape[2])
    return lax.dynamic_slice(padded, (0, chip * 2 * plan.strip, 0), shape)


def freq_pairs(groups, tiles, flip):
    pairs = []
    for g in range(groups):
        for t in range(tiles):
            to = g + 1 if t % 2 == 0 else g - 1
            target = (to, t ^ flip) if 0 <= to < groups else (g, (t + 2) % tiles)
            pairs.append((g * tiles + t, target[0] * tiles + target[1]))
    return pairs


def gathered(plan, plane, tiles):
    if tiles & (tiles - 1):
        held = lax.all_gather(plane, "tile", axis=0, tiled=True)
        return chip_rows(plan, held, lax.axis_index("tile") // 2)
    tile, size, held = lax.axis_index("tile"), 1, plane
    while size < tiles:
        taken = lax.ppermute(held, "tile", [(t, t ^ (2 * size - 1)) for t in range(tiles)])
        held = in_order((tile // size) % 2 == 1, held, taken)
        size *= 2
    return chip_rows(plan, held, tile // 2)


def some_planes(planes, tile):
    begin = (jnp.where(faces_lower(tile), planes.shape[0] - 3, 0), 0, 0)
    return lax.dynamic_slice(planes, begin, (3, *planes.shape[1:]))


def exchanged(plan, plane, groups, tiles, weights, make_bands):
    axes, tile = ("freq", "tile"), lax.axis_index("tile")
    if tiles != 4:
        own = gathered(plan, plane, tiles)
        message = some_planes(own, tile + 1)
        return own, lax.ppermute(message, axes, freq_pairs(groups, tiles, 1)), make_bands(weights)
    taken = lax.ppermute(plane, "tile", [(t, t ^ 1) for t in range(tiles)])
    pair = in_order(tile % 2 == 1, plane, taken)
    chip = tile // 2
    mine, theirs = chip_rows(plan, pair, chip), chip_rows(plan, pair, 1 - chip)
    aside = lax.ppermute(theirs, axes, freq_pairs(groups, tiles, 3))
    ahead = lax.ppermute(mine, axes, freq_pairs(groups, tiles, 1))
    across = lax.ppermute(theirs, "tile", [(t, t ^ 3) for t in range(tiles)])
    aside, *weights = lax.optimization_barrier((aside, *weights))
    bands = make_bands(weights)
    ahead, *bands = lax.optimization_barrier((ahead, *bands))
    own = in_order(chip == 1, mine, across)
    return own, some_planes(in_order(chip == 1, ahead, aside), tile), bands


def even_odd(cube):
    width = cube.shape[2]
    row = lax.broadcasted_iota(jnp.int32, (width, width), 0)
    col = lax.broadcasted_iota(jnp.int32, (width, width), 1)
    order = (row == 2 * (col % (width // 2)) + col // (width // 2)).astype(BF)
    return jnp.einsum("pyx,xw->pyw", cube.astype(BF), order, preferred_element_type=F32).astype(BF)


def body(sky_cube, kernel_one, bias_one, kernel_two, bias_two, kernel_three, bias_three):
    tiles, groups = lax.axis_size("tile"), lax.axis_size("freq")
    strip = sky_cube.shape[1] // tiles
    depth = tiles * sky_cube.shape[0]
    c1, c2, c3 = (kernel.shape[0] for kernel in (kernel_one, kernel_two, kernel_three))
    plan = Plan(strip, depth, c1, c2, c3)
    tile = lax.axis_index("tile")

    w1 = jnp.transpose(kernel_one[:, 0], (1, 2, 3, 0))
    w2 = jnp.transpose(kernel_two, (2, 3, 4, 0, 1))
    w3 = jnp.transpose(kernel_three, (2, 3, 4, 1, 0))

    params = pltpu.CompilerParams(vmem_limit_bytes=32 * 2**20)

    def make_bands(weights):
        bias_one, bias_two, bias_three, w1, w2, w3 = weights
        bands_12 = pl.pallas_call(
            functools.partial(bands_12_kernel, plan),
            name="bands_12",
            out_shape=[
                jax.ShapeDtypeStruct((plan.n1, plan.k1), BF),
                jax.ShapeDtypeStruct((3 * plan.out2, plan.k2), BF),
                jax.ShapeDtypeStruct((c1, 128), F32),
                jax.ShapeDtypeStruct((c2, 128), F32),
                jax.ShapeDtypeStruct((c3, plan.r3, 128), F32),
            ],
            in_specs=[VM] * 5,
            out_specs=[VM] * 5,
            compiler_params=params,
        )(bias_one, bias_two, bias_three, w1, w2)
        bands_3 = pl.pallas_call(
            functools.partial(bands_3_kernel, plan),
            name="bands_3",
            out_shape=jax.ShapeDtypeStruct((2, 3 * plan.out3, plan.k3), BF),
            in_specs=[VM],
            out_specs=VM,
            compiler_params=params,
        )(w3)
        return (*bands_12, bands_3)

    own, got, weights = exchanged(
        plan, even_odd(sky_cube), groups, tiles, (bias_one[None], bias_two[None], bias_three[None], w1, w2, w3), make_bands
    )
    t1, t2, b1, b2, b3, t3 = weights
    other = lax.ppermute(got, "tile", [(t, t ^ 1) for t in range(tiles)])
    done, middle = pl.pallas_call(
        functools.partial(early_kernel, plan),
        name="early",
        out_shape=[
            jax.ShapeDtypeStruct((plan.planes2, plan.n2, 128), BF),
            jax.ShapeDtypeStruct((depth - 2, plan.n1, 128), BF),
        ],
        in_specs=[VM] * 6,
        out_specs=[VM] * 2,
        compiler_params=params,
    )(own, got, t1, t2, b1, b2)
    other, done = lax.optimization_barrier((other, done))
    return pl.pallas_call(
        functools.partial(late_kernel, plan),
        name="late",
        out_shape=jax.ShapeDtypeStruct((c3, depth // 2, plan.r3, sky_cube.shape[2] // 2), BF),
        in_specs=[VM] * 10,
        out_specs=VM,
        compiler_params=params,
    )(own, other, middle, done, t1, t2, b1, b2, t3, b3)


def solution(mesh):
    return jax.shard_map(
        body,
        mesh=mesh,
        in_specs=(P(("freq", "tile"), None, None), P(), P(), P(), P(), P(), P()),
        out_specs=P(None, "freq", "tile", None),
        check_vma=False,
    )
```

```python
import functools

import jax
import jax.numpy as jnp
from jax import lax
from jax.experimental import pallas as pl
from jax.experimental.pallas import tpu as pltpu
from jax.sharding import PartitionSpec as P

BF = jnp.bfloat16
F32 = jnp.float32
VM = pl.BlockSpec(memory_space=pltpu.VMEM)


def even(n):
    return n + n % 2


def up_to(n, unit):
    return -(-n // unit) * unit


class Plan:
    def __init__(self, strip, depth, c1, c2, c3):
        self.strip, self.depth, self.c1, self.c2, self.c3 = strip, depth, c1, c2, c3
        self.rim = 4
        self.slots = strip + 2 * self.rim
        self.span = 2 * strip + 2 * self.rim
        self.plane_k = up_to(3 * self.slots, 16)
        self.k1 = up_to(3 * self.plane_k, 256)
        self.block2, self.block3 = 6, 4
        self.r2 = up_to(strip + 1, self.block2)
        self.r1 = self.r2 + 2
        self.r3 = strip // 2
        self.n1, self.n2 = self.r1 * c1, self.r2 * c2
        self.in2, self.out2 = (self.block2 + 2) * c1, self.block2 * c2
        self.in3, self.out3 = (2 * self.block3 + 2) * c2, self.block3 * c3
        self.k2, self.k3 = up_to(3 * self.in2, 256), up_to(3 * self.in3, 256)
        self.planes1, self.planes2 = depth + 3, depth + 1


def leaky_relu(values):
    return jnp.maximum(values, 0.1 * values)


def faces_lower(tile):
    return tile % 2 == 1


def column_of(bias_ref, rows):
    at = lax.broadcasted_iota(jnp.int32, (rows, rows), 0)
    lane = lax.broadcasted_iota(jnp.int32, (rows, rows), 1)
    spread = jnp.where(at == lane, jnp.broadcast_to(bias_ref[...], (rows, rows)), 0.0)
    return jnp.broadcast_to(jnp.sum(spread, axis=1, keepdims=True), (rows, 128))


def ones_where(hit):
    return hit.astype(F32).astype(BF)


def dot_over_rows(left, right):
    return lax.dot_general(left, right, (((0,), (0,)), ((), ())), preferred_element_type=F32)


def rolled(x, by):
    return pltpu.roll(x, by, 1) if by else x


def bands_kernel(plan, bias1, bias2, bias3, w1, w2, w3, t1, t2, b1, b2, b3, t3):
    c1, c2 = plan.c1, plan.c2
    slots = plan.slots
    bands_3(plan, w3, t3)
    b1[...] = column_of(bias1, c1)
    b2[...] = column_of(bias2, c2)
    column = column_of(bias3, plan.c3)
    b3[...] = jnp.broadcast_to(column[:, None], b3.shape)
    tap = lax.broadcasted_iota(jnp.int32, (3, plan.k1), 0)
    lane = lax.broadcasted_iota(jnp.int32, (3, plan.k1), 1)
    taps = []
    for b in range(3):
        taps.append(
            sum(
                dot_over_rows(w1[a, b], ones_where(lane == a * plan.plane_k + tap * slots))
                for a in range(3)
            )
        )
    base = sum(rolled(taps[b], b) for b in range(3))
    for y in range(0, plan.r1, 2):
        rows = [rolled(base, y + k + plan.rim - 3) for k in range(2)]
        t1[y * c1 : (y + 2) * c1, :] = jnp.concatenate(rows, axis=0).astype(BF)

    for c in range(3):
        parts = [jnp.zeros((c2, 128), F32) for _ in range(plan.k2 // 128)]
        for a in range(3):
            for b in range(3):
                at = a * plan.in2 + b * c1
                tile = w2[a, b, c].astype(F32)
                tile = jnp.concatenate([tile, jnp.zeros((c2, 128 - c1), F32)], axis=1)
                parts[at // 128] += rolled(tile, at % 128)
        base = jnp.concatenate(parts, axis=1)
        for y in range(0, plan.block2, 2):
            rows = [rolled(base, (y + k) * c1) for k in range(2)]
            at = c * plan.out2 + y * c2
            t2[at : at + 2 * c2, :] = jnp.concatenate(rows, axis=0).astype(BF)


def parts_of(count, *sizes):
    at, digits = lax.broadcasted_iota(jnp.int32, (count, 1), 0), []
    for size in reversed(sizes):
        digits.append(lax.rem(at, size))
        at = lax.div(at, size)
    return at, *reversed(digits)


def bands_3(plan, w3, t3):
    c2, c3, rows = plan.c2, plan.c3, plan.block3
    n3 = plan.out3
    odd, pair, which, y = parts_of(2 * n3, c3 // 2, 2, rows)
    source = lax.broadcasted_iota(jnp.int32, (2 * n3, n3), 1)
    turn = ones_where(source == y * c3 + 2 * pair + lax.rem(which + odd, 2))
    a, b, i = parts_of(9 * c2, 3, c2)
    lane = lax.broadcasted_iota(jnp.int32, (9 * c2, plan.k3), 1)
    spread = ones_where(lane == a * plan.in3 + b * c2 + i)
    for c in range(3):
        taken = w3[:, :, c].astype(F32).reshape(9 * c2, c3).astype(BF)
        base = dot_over_rows(taken, spread)
        stacked = [rolled(base, 2 * y * c2) for y in range(rows)]
        stacked = jnp.concatenate(stacked, axis=0).astype(BF)
        both = jnp.dot(turn, stacked, preferred_element_type=F32).astype(BF)
        for odd in range(2):
            t3[odd, c * n3 : (c + 1) * n3, :] = both[odd * n3 : (odd + 1) * n3]


class Place:
    def __init__(self):
        freq, tile = lax.axis_index("freq"), lax.axis_index("tile")
        self.second = lax.rem(tile, 2) == 1
        self.faces_lower = faces_lower(tile)
        self.has_lower, self.has_upper = freq > 0, freq < lax.axis_size("freq") - 1
        self.has_above, self.has_below = tile > 0, tile < lax.axis_size("tile") - 1


def lane_of(x):
    return lax.broadcasted_iota(jnp.int32, x.shape, 1)


def turned(x, by):
    return pltpu.roll(x, by, 1)


def column_taps(x):
    lane, zero, half = lane_of(x), jnp.zeros_like(x), turned(x, 64)
    before = jnp.where(lane < 64, turned(x, 65), half)
    after = jnp.where(lane < 64, half, turned(x, 63))
    return jnp.where(lane == 0, zero, before), x, jnp.where(lane == 127, zero, after)


def sum_of_taps(before, here, after):
    lane, zero = lane_of(here), jnp.zeros_like(here)
    half = turned(jnp.where(lane < 64, before, after), 64)
    rest = jnp.where(lane < 64, turned(before, 65), turned(after, 63))
    return here + half + jnp.where((lane == 0) | (lane == 127), zero, rest)


def sum_of_even_taps(before, here, after):
    lane, zero = lane_of(here), jnp.zeros_like(here)
    return here + turned(after, 64) + jnp.where(lane == 0, zero, turned(before, 65))


def own_rows(plan, place, ref, plane):
    rows = ref[plane].astype(F32)
    return jnp.where(place.second, rows[plan.strip :], rows[: plan.slots])


def rim_rows(plan, place, ref, plane, inside):
    return jnp.where(inside, own_rows(plan, place, ref, plane), 0.0)


def piece(plan, rows):
    pad = jnp.zeros((plan.plane_k - 3 * plan.slots, 128), F32)
    return jnp.concatenate([*column_taps(rows), pad], axis=0).astype(BF)


def in_twos(planes):
    planes = list(planes)
    return [planes[i : i + 2] for i in range(0, len(planes), 2)]


def layer_one(plan, place, pieces, planes, t1, b1):
    pad = jnp.zeros((plan.k1 - 3 * plan.plane_k, 128), BF)
    strip, made = plan.strip, {}
    for chunk in in_twos(planes):
        x1 = [jnp.concatenate([*pieces[p : p + 3], pad], axis=0) for p in chunk]
        sums = jnp.dot(t1[...], jnp.concatenate(x1, axis=1), preferred_element_type=F32)
        for i, p in enumerate(chunk):
            v = sums[:, i * 128 : (i + 1) * 128].reshape(plan.r1, plan.c1, 128)
            v = leaky_relu(v + b1[...])
            if p < 2:
                v = jnp.where(place.has_lower, v, 0.0)
            if p == plan.planes1 - 1:
                v = jnp.where(place.has_upper, v, 0.0)
            v = jnp.concatenate(
                [
                    jnp.where(place.has_above, v[:2], 0.0),
                    v[2 : strip + 2],
                    jnp.where(place.has_below, v[strip + 2 :], 0.0),
                ],
                axis=0,
            )
            made[p] = v.reshape(plan.n1, 128).astype(BF)
    return made


def blocks_of(planes, rows, step, size, k):
    parts = [plane[step * k : step * k + size] for plane in planes]
    return jnp.concatenate(parts + [jnp.zeros((rows - len(parts) * size, 128), BF)], axis=0)


def layer_two(plan, place, layer_one, planes, t2, b2):
    out2, blocks = plan.out2, {}
    for chunk in in_twos((q, k) for q in planes for k in range(plan.r2 // plan.block2)):
        x = []
        for q, k in chunk:
            x.append(blocks_of([layer_one(q + a) for a in range(3)], plan.k2, out2, plan.in2, k))
        sums = jnp.dot(t2[...], jnp.concatenate(x, axis=1), preferred_element_type=F32)
        for i, (q, k) in enumerate(chunk):
            taps = [sums[c * out2 : (c + 1) * out2, i * 128 : (i + 1) * 128] for c in range(3)]
            v = sum_of_taps(*taps).reshape(plan.block2, plan.c2, 128)
            v = leaky_relu(v + b2[...])
            if q == 0:
                v = jnp.where(place.has_lower, v, 0.0)
            if k == 0:
                v = jnp.concatenate([jnp.where(place.has_above, v[:1], 0.0), v[1:]], axis=0)
            blocks.setdefault(q, []).append(v.reshape(out2, 128).astype(BF))
    return {q: jnp.concatenate(parts, axis=0) for q, parts in blocks.items()}


def layer_three(plan, layer_two, t3, b3, out):
    n3, rows = plan.out3, plan.block3
    for chunk in in_twos(range(plan.depth // 2)):
        for y in range(0, plan.r3, 2 * rows):
            halves = []
            for odd in range(2):
                x = []
                for f in chunk:
                    planes = [layer_two(2 * f + a) for a in range(3)]
                    x.append(blocks_of(planes, plan.k3, 2 * rows * plan.c2, plan.in3, y // rows + odd))
                x = jnp.concatenate(x, axis=1)
                halves.append(jnp.dot(t3[odd], x, preferred_element_type=F32))
            for i, f in enumerate(chunk):
                first, second = (
                    sum_of_even_taps(
                        *(half[c * n3 : (c + 1) * n3, i * 128 : (i + 1) * 128] for c in range(3))
                    ).reshape(plan.c3 // 2, 2 * rows, 128)
                    for half in halves
                )
                sub = lax.broadcasted_iota(jnp.int32, first.shape, 1)
                one = jnp.where(sub < rows, first, second)
                other = jnp.where(sub < rows, second, first)
                other = jnp.concatenate([other[:, rows:], other[:, :rows]], axis=1)
                v = jnp.stack([one, other], axis=1).reshape(plan.c3, 2 * rows, 128)
                v = leaky_relu(v + b3[:, y : y + 2 * rows])
                out[:, f, y : y + 2 * rows] = v[:, :, :64].astype(BF)


def lower_half(plan, place, own, halo, t1, t2, b1, b2, middle=None):
    pieces = [piece(plan, rim_rows(plan, place, halo, p, place.has_lower)) for p in range(3)]
    pieces += [piece(plan, own_rows(plan, place, own, p)) for p in range(plan.depth if middle is None else 2)]
    made = layer_one(plan, place, pieces, range(plan.depth + 1 if middle is None else 3), t1, b1)
    some = lambda p: made[p] if p in made else middle[p - 3]
    return layer_two(plan, place, some, range(3), t2, b2), made


def upper_half(plan, place, own, halo, t1, t2, b1, b2, middle=None):
    depth = plan.depth
    first = 0 if middle is None else depth - 2
    pieces = [None] * (3 + first)
    pieces += [piece(plan, own_rows(plan, place, own, p)) for p in range(first, depth)]
    pieces += [piece(plan, rim_rows(plan, place, halo, p, place.has_upper)) for p in range(2)]
    made = layer_one(plan, place, pieces, range(3 + first, depth + 3), t1, b1)
    some = lambda p: made[p] if p in made else middle[p - 3]
    return layer_two(plan, place, some, range(3, depth + 1), t2, b2), made


def early_kernel(plan, own, got, t1, t2, b1, b2, done, middle):
    place = Place()

    def run(half):
        planes, made = half(plan, place, own, got, t1, t2, b1, b2)
        for q, v in planes.items():
            done[q] = v
        for p in range(3, plan.depth + 1):
            middle[p - 3] = made[p]

    pl.when(place.faces_lower)(lambda: run(lower_half))
    pl.when(jnp.logical_not(place.faces_lower))(lambda: run(upper_half))


def late_kernel(plan, own, other, middle, done, t1, t2, b1, b2, t3, b3, out):
    place = Place()

    def run(half):
        late, _ = half(plan, place, own, other, t1, t2, b1, b2, middle)
        layer_three(plan, lambda q: late[q] if q in late else done[q], t3, b3, out)

    pl.when(place.faces_lower)(lambda: run(upper_half))
    pl.when(jnp.logical_not(place.faces_lower))(lambda: run(lower_half))


def in_order(upper, held, taken):
    return jnp.where(
        upper,
        jnp.concatenate([taken, held], axis=0),
        jnp.concatenate([held, taken], axis=0),
    )


def chip_rows(plan, planes, chip):
    padded = jnp.pad(planes, ((0, 0), (plan.rim, plan.rim), (0, 0)))
    shape = (planes.shape[0], plan.span, planes.shape[2])
    return lax.dynamic_slice(padded, (0, chip * 2 * plan.strip, 0), shape)


def freq_pairs(groups, tiles, flip):
    pairs = []
    for g in range(groups):
        for t in range(tiles):
            to = g + 1 if t % 2 == 0 else g - 1
            target = (to, t ^ flip) if 0 <= to < groups else (g, (t + 2) % tiles)
            pairs.append((g * tiles + t, target[0] * tiles + target[1]))
    return pairs


def gathered(plan, plane, tiles):
    if tiles & (tiles - 1):
        held = lax.all_gather(plane, "tile", axis=0, tiled=True)
        return chip_rows(plan, held, lax.axis_index("tile") // 2)
    tile, size, held = lax.axis_index("tile"), 1, plane
    while size < tiles:
        taken = lax.ppermute(held, "tile", [(t, t ^ (2 * size - 1)) for t in range(tiles)])
        held = in_order((tile // size) % 2 == 1, held, taken)
        size *= 2
    return chip_rows(plan, held, tile // 2)


def some_planes(planes, tile):
    begin = (jnp.where(faces_lower(tile), planes.shape[0] - 3, 0), 0, 0)
    return lax.dynamic_slice(planes, begin, (3, *planes.shape[1:]))


def exchanged(plan, plane, groups, tiles, weights, make_bands):
    axes, tile = ("freq", "tile"), lax.axis_index("tile")
    if tiles != 4:
        own = gathered(plan, plane, tiles)
        message = some_planes(own, tile + 1)
        return own, lax.ppermute(message, axes, freq_pairs(groups, tiles, 1)), make_bands(weights)
    taken = lax.ppermute(plane, "tile", [(t, t ^ 1) for t in range(tiles)])
    pair = in_order(tile % 2 == 1, plane, taken)
    chip = tile // 2
    mine, theirs = chip_rows(plan, pair, chip), chip_rows(plan, pair, 1 - chip)
    ahead = lax.ppermute(mine, axes, freq_pairs(groups, tiles, 1))
    aside = lax.ppermute(theirs, axes, freq_pairs(groups, tiles, 3))
    across = lax.ppermute(theirs, "tile", [(t, t ^ 3) for t in range(tiles)])
    ahead, *weights = lax.optimization_barrier((ahead, *weights))
    bands = make_bands(weights)
    aside, *bands = lax.optimization_barrier((aside, *bands))
    own = in_order(chip == 1, mine, across)
    return own, some_planes(in_order(chip == 1, ahead, aside), tile), bands


def even_odd(cube):
    width = cube.shape[2]
    row = lax.broadcasted_iota(jnp.int32, (width, width), 0)
    col = lax.broadcasted_iota(jnp.int32, (width, width), 1)
    order = (row == 2 * (col % (width // 2)) + col // (width // 2)).astype(BF)
    return jnp.einsum("pyx,xw->pyw", cube.astype(BF), order, preferred_element_type=F32).astype(BF)


def body(sky_cube, kernel_one, bias_one, kernel_two, bias_two, kernel_three, bias_three):
    tiles, groups = lax.axis_size("tile"), lax.axis_size("freq")
    strip = sky_cube.shape[1] // tiles
    depth = tiles * sky_cube.shape[0]
    c1, c2, c3 = (kernel.shape[0] for kernel in (kernel_one, kernel_two, kernel_three))
    plan = Plan(strip, depth, c1, c2, c3)
    tile = lax.axis_index("tile")

    w1 = jnp.transpose(kernel_one[:, 0], (1, 2, 3, 0))
    w2 = jnp.transpose(kernel_two, (2, 3, 4, 0, 1))
    w3 = jnp.transpose(kernel_three, (2, 3, 4, 1, 0))

    params = pltpu.CompilerParams(vmem_limit_bytes=32 * 2**20)

    def make_bands(weights):
        return pl.pallas_call(
            functools.partial(bands_kernel, plan),
            name="bands",
            out_shape=[
                jax.ShapeDtypeStruct((plan.n1, plan.k1), BF),
                jax.ShapeDtypeStruct((3 * plan.out2, plan.k2), BF),
                jax.ShapeDtypeStruct((c1, 128), F32),
                jax.ShapeDtypeStruct((c2, 128), F32),
                jax.ShapeDtypeStruct((c3, plan.r3, 128), F32),
                jax.ShapeDtypeStruct((2, 3 * plan.out3, plan.k3), BF),
            ],
            in_specs=[VM] * 6,
            out_specs=[VM] * 6,
            compiler_params=params,
        )(*weights)

    own, got, weights = exchanged(
        plan, even_odd(sky_cube), groups, tiles, (bias_one[None], bias_two[None], bias_three[None], w1, w2, w3), make_bands
    )
    t1, t2, b1, b2, b3, t3 = weights
    other = lax.ppermute(got, "tile", [(t, t ^ 1) for t in range(tiles)])
    done, middle = pl.pallas_call(
        functools.partial(early_kernel, plan),
        name="early",
        out_shape=[
            jax.ShapeDtypeStruct((plan.planes2, plan.n2, 128), BF),
            jax.ShapeDtypeStruct((depth - 2, plan.n1, 128), BF),
        ],
        in_specs=[VM] * 6,
        out_specs=[VM] * 2,
        compiler_params=params,
    )(own, got, t1, t2, b1, b2)
    other, done = lax.optimization_barrier((other, done))
    return pl.pallas_call(
        functools.partial(late_kernel, plan),
        name="late",
        out_shape=jax.ShapeDtypeStruct((c3, depth // 2, plan.r3, sky_cube.shape[2] // 2), BF),
        in_specs=[VM] * 10,
        out_specs=VM,
        compiler_params=params,
    )(own, other, middle, done, t1, t2, b1, b2, t3, b3)


def solution(mesh):
    return jax.shard_map(
        body,
        mesh=mesh,
        in_specs=(P(("freq", "tile"), None, None), P(), P(), P(), P(), P(), P()),
        out_specs=P(None, "freq", "tile", None),
        check_vma=False,
    )
```

```python
import functools

import jax
import jax.numpy as jnp
from jax import lax
from jax.experimental import pallas as pl
from jax.experimental.pallas import tpu as pltpu
from jax.sharding import PartitionSpec as P

BF = jnp.bfloat16
F32 = jnp.float32
VM = pl.BlockSpec(memory_space=pltpu.VMEM)


def even(n):
    return n + n % 2


def up_to(n, unit):
    return -(-n // unit) * unit


class Plan:
    def __init__(self, strip, depth, c1, c2, c3):
        self.strip, self.depth, self.c1, self.c2, self.c3 = strip, depth, c1, c2, c3
        self.rim = 4
        self.slots = strip + 2 * self.rim
        self.span = 2 * strip + 2 * self.rim
        self.plane_k = up_to(3 * self.slots, 16)
        self.k1 = up_to(3 * self.plane_k, 256)
        self.block2, self.block3 = 6, 4
        self.r2 = up_to(strip + 1, self.block2)
        self.r1 = self.r2 + 2
        self.r3 = strip // 2
        self.n1, self.n2 = self.r1 * c1, self.r2 * c2
        self.in2, self.out2 = (self.block2 + 2) * c1, self.block2 * c2
        self.in3, self.out3 = (2 * self.block3 + 2) * c2, self.block3 * c3
        self.k2, self.k3 = up_to(3 * self.in2, 256), up_to(3 * self.in3, 256)
        self.planes1, self.planes2 = depth + 3, depth + 1


def leaky_relu(values):
    return jnp.maximum(values, 0.1 * values)


def faces_lower(tile):
    return tile % 2 == 1


def column_of(bias_ref, rows):
    at = lax.broadcasted_iota(jnp.int32, (rows, rows), 0)
    lane = lax.broadcasted_iota(jnp.int32, (rows, rows), 1)
    spread = jnp.where(at == lane, jnp.broadcast_to(bias_ref[...], (rows, rows)), 0.0)
    return jnp.broadcast_to(jnp.sum(spread, axis=1, keepdims=True), (rows, 128))


def ones_where(hit):
    return hit.astype(F32).astype(BF)


def dot_over_rows(left, right):
    return lax.dot_general(left, right, (((0,), (0,)), ((), ())), preferred_element_type=F32)


def rolled(x, by):
    return pltpu.roll(x, by, 1) if by else x


def bands_kernel(plan, bias1, bias2, bias3, w1, w2, w3, t1, t2, b1, b2, b3, t3):
    c1, c2 = plan.c1, plan.c2
    slots = plan.slots
    bands_3(plan, w3, t3)
    b1[...] = column_of(bias1, c1)
    b2[...] = column_of(bias2, c2)
    column = column_of(bias3, plan.c3)
    b3[...] = jnp.broadcast_to(column[:, None], b3.shape)
    tap = lax.broadcasted_iota(jnp.int32, (3, plan.k1), 0)
    lane = lax.broadcasted_iota(jnp.int32, (3, plan.k1), 1)
    taps = []
    for b in range(3):
        taps.append(
            sum(
                dot_over_rows(w1[a, b], ones_where(lane == a * plan.plane_k + tap * slots))
                for a in range(3)
            )
        )
    base = sum(rolled(taps[b], b) for b in range(3))
    for y in range(0, plan.r1, 2):
        rows = [rolled(base, y + k + plan.rim - 3) for k in range(2)]
        t1[y * c1 : (y + 2) * c1, :] = jnp.concatenate(rows, axis=0).astype(BF)

    for c in range(3):
        parts = [jnp.zeros((c2, 128), F32) for _ in range(plan.k2 // 128)]
        for a in range(3):
            for b in range(3):
                at = a * plan.in2 + b * c1
                tile = w2[a, b, c].astype(F32)
                tile = jnp.concatenate([tile, jnp.zeros((c2, 128 - c1), F32)], axis=1)
                parts[at // 128] += rolled(tile, at % 128)
        base = jnp.concatenate(parts, axis=1)
        for y in range(0, plan.block2, 2):
            rows = [rolled(base, (y + k) * c1) for k in range(2)]
            at = c * plan.out2 + y * c2
            t2[at : at + 2 * c2, :] = jnp.concatenate(rows, axis=0).astype(BF)


def parts_of(count, *sizes):
    at, digits = lax.broadcasted_iota(jnp.int32, (count, 1), 0), []
    for size in reversed(sizes):
        digits.append(lax.rem(at, size))
        at = lax.div(at, size)
    return at, *reversed(digits)


def bands_3(plan, w3, t3):
    c2, c3, rows = plan.c2, plan.c3, plan.block3
    n3 = plan.out3
    odd, pair, which, y = parts_of(2 * n3, c3 // 2, 2, rows)
    source = lax.broadcasted_iota(jnp.int32, (2 * n3, n3), 1)
    turn = ones_where(source == y * c3 + 2 * pair + lax.rem(which + odd, 2))
    a, b, i = parts_of(9 * c2, 3, c2)
    lane = lax.broadcasted_iota(jnp.int32, (9 * c2, plan.k3), 1)
    spread = ones_where(lane == a * plan.in3 + b * c2 + i)
    for c in range(3):
        taken = w3[:, :, c].astype(F32).reshape(9 * c2, c3).astype(BF)
        base = dot_over_rows(taken, spread)
        stacked = [rolled(base, 2 * y * c2) for y in range(rows)]
        stacked = jnp.concatenate(stacked, axis=0).astype(BF)
        both = jnp.dot(turn, stacked, preferred_element_type=F32).astype(BF)
        for odd in range(2):
            t3[odd, c * n3 : (c + 1) * n3, :] = both[odd * n3 : (odd + 1) * n3]


class Place:
    def __init__(self):
        freq, tile = lax.axis_index("freq"), lax.axis_index("tile")
        self.second = lax.rem(tile, 2) == 1
        self.faces_lower = faces_lower(tile)
        self.has_lower, self.has_upper = freq > 0, freq < lax.axis_size("freq") - 1
        self.has_above, self.has_below = tile > 0, tile < lax.axis_size("tile") - 1


def lane_of(x):
    return lax.broadcasted_iota(jnp.int32, x.shape, 1)


def turned(x, by):
    return pltpu.roll(x, by, 1)


def column_taps(x):
    lane, zero, half = lane_of(x), jnp.zeros_like(x), turned(x, 64)
    before = jnp.where(lane < 64, turned(x, 65), half)
    after = jnp.where(lane < 64, half, turned(x, 63))
    return jnp.where(lane == 0, zero, before), x, jnp.where(lane == 127, zero, after)


def sum_of_taps(before, here, after):
    lane, zero = lane_of(here), jnp.zeros_like(here)
    half = turned(jnp.where(lane < 64, before, after), 64)
    rest = jnp.where(lane < 64, turned(before, 65), turned(after, 63))
    return here + half + jnp.where((lane == 0) | (lane == 127), zero, rest)


def sum_of_even_taps(before, here, after):
    lane, zero = lane_of(here), jnp.zeros_like(here)
    return here + turned(after, 64) + jnp.where(lane == 0, zero, turned(before, 65))


def own_rows(plan, place, ref, plane):
    rows = ref[plane].astype(F32)
    return jnp.where(place.second, rows[plan.strip :], rows[: plan.slots])


def rim_rows(plan, place, ref, plane, inside):
    return jnp.where(inside, own_rows(plan, place, ref, plane), 0.0)


def piece(plan, rows):
    pad = jnp.zeros((plan.plane_k - 3 * plan.slots, 128), F32)
    return jnp.concatenate([*column_taps(rows), pad], axis=0).astype(BF)


def in_twos(planes):
    planes = list(planes)
    return [planes[i : i + 2] for i in range(0, len(planes), 2)]


def layer_one(plan, place, pieces, planes, t1, b1):
    pad = jnp.zeros((plan.k1 - 3 * plan.plane_k, 128), BF)
    strip, made = plan.strip, {}
    for chunk in in_twos(planes):
        x1 = [jnp.concatenate([*pieces[p : p + 3], pad], axis=0) for p in chunk]
        sums = jnp.dot(t1[...], jnp.concatenate(x1, axis=1), preferred_element_type=F32)
        for i, p in enumerate(chunk):
            v = sums[:, i * 128 : (i + 1) * 128].reshape(plan.r1, plan.c1, 128)
            v = leaky_relu(v + b1[...])
            if p < 2:
                v = jnp.where(place.has_lower, v, 0.0)
            if p == plan.planes1 - 1:
                v = jnp.where(place.has_upper, v, 0.0)
            v = jnp.concatenate(
                [
                    jnp.where(place.has_above, v[:2], 0.0),
                    v[2 : strip + 2],
                    jnp.where(place.has_below, v[strip + 2 :], 0.0),
                ],
                axis=0,
            )
            made[p] = v.reshape(plan.n1, 128).astype(BF)
    return made


def blocks_of(planes, rows, step, size, k):
    parts = [plane[step * k : step * k + size] for plane in planes]
    return jnp.concatenate(parts + [jnp.zeros((rows - len(parts) * size, 128), BF)], axis=0)


def layer_two(plan, place, layer_one, planes, t2, b2):
    out2, blocks = plan.out2, {}
    for chunk in in_twos((q, k) for q in planes for k in range(plan.r2 // plan.block2)):
        x = []
        for q, k in chunk:
            x.append(blocks_of([layer_one(q + a) for a in range(3)], plan.k2, out2, plan.in2, k))
        sums = jnp.dot(t2[...], jnp.concatenate(x, axis=1), preferred_element_type=F32)
        for i, (q, k) in enumerate(chunk):
            taps = [sums[c * out2 : (c + 1) * out2, i * 128 : (i + 1) * 128] for c in range(3)]
            v = sum_of_taps(*taps).reshape(plan.block2, plan.c2, 128)
            v = leaky_relu(v + b2[...])
            if q == 0:
                v = jnp.where(place.has_lower, v, 0.0)
            if k == 0:
                v = jnp.concatenate([jnp.where(place.has_above, v[:1], 0.0), v[1:]], axis=0)
            blocks.setdefault(q, []).append(v.reshape(out2, 128).astype(BF))
    return {q: jnp.concatenate(parts, axis=0) for q, parts in blocks.items()}


def layer_three(plan, layer_two, t3, b3, out):
    n3, rows = plan.out3, plan.block3
    for f in range(plan.depth // 2):
        planes = [layer_two(2 * f + a) for a in range(3)]
        for y in range(0, plan.r3, 2 * rows):
            first, second = (
                jnp.dot(
                    t3[odd],
                    blocks_of(planes, plan.k3, 2 * rows * plan.c2, plan.in3, y // rows + odd),
                    preferred_element_type=F32,
                )
                for odd in range(2)
            )
            first, second = (
                sum_of_even_taps(*(half[c * n3 : (c + 1) * n3] for c in range(3))).reshape(
                    plan.c3 // 2, 2 * rows, 128
                )
                for half in (first, second)
            )
            sub = lax.broadcasted_iota(jnp.int32, first.shape, 1)
            one = jnp.where(sub < rows, first, second)
            other = jnp.where(sub < rows, second, first)
            other = jnp.concatenate([other[:, rows:], other[:, :rows]], axis=1)
            v = jnp.stack([one, other], axis=1).reshape(plan.c3, 2 * rows, 128)
            v = leaky_relu(v + b3[:, y : y + 2 * rows])
            out[:, f, y : y + 2 * rows] = v[:, :, :64].astype(BF)


def lower_half(plan, place, own, halo, t1, t2, b1, b2, middle=None):
    pieces = [piece(plan, rim_rows(plan, place, halo, p, place.has_lower)) for p in range(3)]
    pieces += [piece(plan, own_rows(plan, place, own, p)) for p in range(plan.depth if middle is None else 2)]
    made = layer_one(plan, place, pieces, range(plan.depth + 1 if middle is None else 3), t1, b1)
    some = lambda p: made[p] if p in made else middle[p - 3]
    return layer_two(plan, place, some, range(3), t2, b2), made


def upper_half(plan, place, own, halo, t1, t2, b1, b2, middle=None):
    depth = plan.depth
    first = 0 if middle is None else depth - 2
    pieces = [None] * (3 + first)
    pieces += [piece(plan, own_rows(plan, place, own, p)) for p in range(first, depth)]
    pieces += [piece(plan, rim_rows(plan, place, halo, p, place.has_upper)) for p in range(2)]
    made = layer_one(plan, place, pieces, range(3 + first, depth + 3), t1, b1)
    some = lambda p: made[p] if p in made else middle[p - 3]
    return layer_two(plan, place, some, range(3, depth + 1), t2, b2), made


def early_kernel(plan, own, got, t1, t2, b1, b2, done, middle):
    place = Place()

    def run(half):
        planes, made = half(plan, place, own, got, t1, t2, b1, b2)
        for q, v in planes.items():
            done[q] = v
        for p in range(3, plan.depth + 1):
            middle[p - 3] = made[p]

    pl.when(place.faces_lower)(lambda: run(lower_half))
    pl.when(jnp.logical_not(place.faces_lower))(lambda: run(upper_half))


def late_kernel(plan, own, other, middle, done, t1, t2, b1, b2, t3, b3, out):
    place = Place()

    def run(half):
        late, _ = half(plan, place, own, other, t1, t2, b1, b2, middle)
        layer_three(plan, lambda q: late[q] if q in late else done[q], t3, b3, out)

    pl.when(place.faces_lower)(lambda: run(upper_half))
    pl.when(jnp.logical_not(place.faces_lower))(lambda: run(lower_half))


def in_order(upper, held, taken):
    return jnp.where(
        upper,
        jnp.concatenate([taken, held], axis=0),
        jnp.concatenate([held, taken], axis=0),
    )


def chip_rows(plan, planes, chip):
    padded = jnp.pad(planes, ((0, 0), (plan.rim, plan.rim), (0, 0)))
    shape = (planes.shape[0], plan.span, planes.shape[2])
    return lax.dynamic_slice(padded, (0, chip * 2 * plan.strip, 0), shape)


def freq_pairs(groups, tiles, flip):
    pairs = []
    for g in range(groups):
        for t in range(tiles):
            to = g + 1 if t % 2 == 0 else g - 1
            target = (to, t ^ flip) if 0 <= to < groups else (g, (t + 2) % tiles)
            pairs.append((g * tiles + t, target[0] * tiles + target[1]))
    return pairs


def gathered(plan, plane, tiles):
    if tiles & (tiles - 1):
        held = lax.all_gather(plane, "tile", axis=0, tiled=True)
        return chip_rows(plan, held, lax.axis_index("tile") // 2)
    tile, size, held = lax.axis_index("tile"), 1, plane
    while size < tiles:
        taken = lax.ppermute(held, "tile", [(t, t ^ (2 * size - 1)) for t in range(tiles)])
        held = in_order((tile // size) % 2 == 1, held, taken)
        size *= 2
    return chip_rows(plan, held, tile // 2)


def some_planes(planes, tile):
    begin = (jnp.where(faces_lower(tile), planes.shape[0] - 3, 0), 0, 0)
    return lax.dynamic_slice(planes, begin, (3, *planes.shape[1:]))


def exchanged(plan, plane, groups, tiles, weights, make_bands):
    axes, tile = ("freq", "tile"), lax.axis_index("tile")
    if tiles != 4:
        own = gathered(plan, even_odd(plane), tiles)
        message = some_planes(own, tile + 1)
        return own, lax.ppermute(message, axes, freq_pairs(groups, tiles, 1)), make_bands(weights)
    taken = lax.ppermute(plane, "tile", [(t, t ^ 1) for t in range(tiles)])
    pair = even_odd(in_order(tile % 2 == 1, plane, taken))
    chip = tile // 2
    mine, theirs = chip_rows(plan, pair, chip), chip_rows(plan, pair, 1 - chip)
    ahead = lax.ppermute(mine, axes, freq_pairs(groups, tiles, 1))
    aside = lax.ppermute(theirs, axes, freq_pairs(groups, tiles, 3))
    across = lax.ppermute(theirs, "tile", [(t, t ^ 3) for t in range(tiles)])
    ahead, *weights = lax.optimization_barrier((ahead, *weights))
    bands = make_bands(weights)
    aside, *bands = lax.optimization_barrier((aside, *bands))
    own = in_order(chip == 1, mine, across)
    return own, some_planes(in_order(chip == 1, ahead, aside), tile), bands


def even_odd(planes):
    width = planes.shape[2]
    row = lax.broadcasted_iota(jnp.int32, (width, width), 0)
    col = lax.broadcasted_iota(jnp.int32, (width, width), 1)
    order = (row == 2 * (col % (width // 2)) + col // (width // 2)).astype(BF)
    return jnp.einsum("pyx,xw->pyw", planes, order, preferred_element_type=F32).astype(BF)


def body(sky_cube, kernel_one, bias_one, kernel_two, bias_two, kernel_three, bias_three):
    tiles, groups = lax.axis_size("tile"), lax.axis_size("freq")
    strip = sky_cube.shape[1] // tiles
    depth = tiles * sky_cube.shape[0]
    c1, c2, c3 = (kernel.shape[0] for kernel in (kernel_one, kernel_two, kernel_three))
    plan = Plan(strip, depth, c1, c2, c3)
    tile = lax.axis_index("tile")

    w1 = jnp.transpose(kernel_one[:, 0], (1, 2, 3, 0))
    w2 = jnp.transpose(kernel_two, (2, 3, 4, 0, 1))
    w3 = jnp.transpose(kernel_three, (2, 3, 4, 1, 0))

    params = pltpu.CompilerParams(vmem_limit_bytes=32 * 2**20)

    def make_bands(weights):
        return pl.pallas_call(
            functools.partial(bands_kernel, plan),
            name="bands",
            out_shape=[
                jax.ShapeDtypeStruct((plan.n1, plan.k1), BF),
                jax.ShapeDtypeStruct((3 * plan.out2, plan.k2), BF),
                jax.ShapeDtypeStruct((c1, 128), F32),
                jax.ShapeDtypeStruct((c2, 128), F32),
                jax.ShapeDtypeStruct((c3, plan.r3, 128), F32),
                jax.ShapeDtypeStruct((2, 3 * plan.out3, plan.k3), BF),
            ],
            in_specs=[VM] * 6,
            out_specs=[VM] * 6,
            compiler_params=params,
        )(*weights)

    own, got, weights = exchanged(
        plan, sky_cube.astype(BF), groups, tiles, (bias_one[None], bias_two[None], bias_three[None], w1, w2, w3), make_bands
    )
    t1, t2, b1, b2, b3, t3 = weights
    other = lax.ppermute(got, "tile", [(t, t ^ 1) for t in range(tiles)])
    done, middle = pl.pallas_call(
        functools.partial(early_kernel, plan),
        name="early",
        out_shape=[
            jax.ShapeDtypeStruct((plan.planes2, plan.n2, 128), BF),
            jax.ShapeDtypeStruct((depth - 2, plan.n1, 128), BF),
        ],
        in_specs=[VM] * 6,
        out_specs=[VM] * 2,
        compiler_params=params,
    )(own, got, t1, t2, b1, b2)
    other, done = lax.optimization_barrier((other, done))
    return pl.pallas_call(
        functools.partial(late_kernel, plan),
        name="late",
        out_shape=jax.ShapeDtypeStruct((c3, depth // 2, plan.r3, sky_cube.shape[2] // 2), BF),
        in_specs=[VM] * 10,
        out_specs=VM,
        compiler_params=params,
    )(own, other, middle, done, t1, t2, b1, b2, t3, b3)


def solution(mesh):
    return jax.shard_map(
        body,
        mesh=mesh,
        in_specs=(P(("freq", "tile"), None, None), P(), P(), P(), P(), P(), P()),
        out_specs=P(None, "freq", "tile", None),
        check_vma=False,
    )
```

```python
import functools

import jax
import jax.numpy as jnp
from jax import lax
from jax.experimental import pallas as pl
from jax.experimental.pallas import tpu as pltpu
from jax.sharding import PartitionSpec as P

BF = jnp.bfloat16
F32 = jnp.float32
VM = pl.BlockSpec(memory_space=pltpu.VMEM)


def even(n):
    return n + n % 2


def up_to(n, unit):
    return -(-n // unit) * unit


class Plan:
    def __init__(self, strip, depth, c1, c2, c3):
        self.strip, self.depth, self.c1, self.c2, self.c3 = strip, depth, c1, c2, c3
        self.rim = 4
        self.slots = strip + 2 * self.rim
        self.span = 2 * strip + 2 * self.rim
        self.plane_k = up_to(3 * self.slots, 16)
        self.k1 = up_to(3 * self.plane_k, 256)
        self.block2, self.block3 = 6, 4
        self.r2 = up_to(strip + 1, self.block2)
        self.r1 = self.r2 + 2
        self.r3 = strip // 2
        self.n1, self.n2 = self.r1 * c1, self.r2 * c2
        self.in2, self.out2 = (self.block2 + 2) * c1, self.block2 * c2
        self.in3, self.out3 = (2 * self.block3 + 2) * c2, self.block3 * c3
        self.k2, self.k3 = up_to(3 * self.in2, 256), up_to(3 * self.in3, 256)
        self.planes1, self.planes2 = depth + 3, depth + 1


def leaky_relu(values):
    return jnp.maximum(values, 0.1 * values)


def faces_lower(tile):
    return tile % 2 == 1


def column_of(bias_ref, rows):
    at = lax.broadcasted_iota(jnp.int32, (rows, rows), 0)
    lane = lax.broadcasted_iota(jnp.int32, (rows, rows), 1)
    spread = jnp.where(at == lane, jnp.broadcast_to(bias_ref[...], (rows, rows)), 0.0)
    return jnp.broadcast_to(jnp.sum(spread, axis=1, keepdims=True), (rows, 128))


def ones_where(hit):
    return hit.astype(F32).astype(BF)


def dot_over_rows(left, right):
    return lax.dot_general(left, right, (((0,), (0,)), ((), ())), preferred_element_type=F32)


def rolled(x, by):
    return pltpu.roll(x, by, 1) if by else x


def bands_kernel(plan, bias1, bias2, bias3, w1, w2, w3, t1, t2, b1, b2, b3, t3):
    c1, c2 = plan.c1, plan.c2
    slots = plan.slots
    bands_3(plan, w3, t3)
    b1[...] = column_of(bias1, c1)
    b2[...] = column_of(bias2, c2)
    column = column_of(bias3, plan.c3)
    b3[...] = jnp.broadcast_to(column[:, None], b3.shape)
    tap = lax.broadcasted_iota(jnp.int32, (3, plan.k1), 0)
    lane = lax.broadcasted_iota(jnp.int32, (3, plan.k1), 1)
    taps = []
    for b in range(3):
        taps.append(
            sum(
                dot_over_rows(w1[a, b], ones_where(lane == a * plan.plane_k + tap * slots))
                for a in range(3)
            )
        )
    base = sum(rolled(taps[b], b) for b in range(3))
    for y in range(0, plan.r1, 2):
        rows = [rolled(base, y + k + plan.rim - 3) for k in range(2)]
        t1[y * c1 : (y + 2) * c1, :] = jnp.concatenate(rows, axis=0).astype(BF)

    for c in range(3):
        parts = [jnp.zeros((c2, 128), F32) for _ in range(plan.k2 // 128)]
        for a in range(3):
            for b in range(3):
                at = a * plan.in2 + b * c1
                tile = w2[a, b, c].astype(F32)
                tile = jnp.concatenate([tile, jnp.zeros((c2, 128 - c1), F32)], axis=1)
                parts[at // 128] += rolled(tile, at % 128)
        base = jnp.concatenate(parts, axis=1)
        for y in range(0, plan.block2, 2):
            rows = [rolled(base, (y + k) * c1) for k in range(2)]
            at = c * plan.out2 + y * c2
            t2[at : at + 2 * c2, :] = jnp.concatenate(rows, axis=0).astype(BF)


def parts_of(count, *sizes):
    at, digits = lax.broadcasted_iota(jnp.int32, (count, 1), 0), []
    for size in reversed(sizes):
        digits.append(lax.rem(at, size))
        at = lax.div(at, size)
    return at, *reversed(digits)


def bands_3(plan, w3, t3):
    c2, c3, rows = plan.c2, plan.c3, plan.block3
    n3 = plan.out3
    odd, pair, which, y = parts_of(2 * n3, c3 // 2, 2, rows)
    source = lax.broadcasted_iota(jnp.int32, (2 * n3, n3), 1)
    turn = ones_where(source == y * c3 + 2 * pair + lax.rem(which + odd, 2))
    a, b, i = parts_of(9 * c2, 3, c2)
    lane = lax.broadcasted_iota(jnp.int32, (9 * c2, plan.k3), 1)
    spread = ones_where(lane == a * plan.in3 + b * c2 + i)
    for c in range(3):
        taken = w3[:, :, c].astype(F32).reshape(9 * c2, c3).astype(BF)
        base = dot_over_rows(taken, spread)
        stacked = [rolled(base, 2 * y * c2) for y in range(rows)]
        stacked = jnp.concatenate(stacked, axis=0).astype(BF)
        both = jnp.dot(turn, stacked, preferred_element_type=F32).astype(BF)
        for odd in range(2):
            t3[odd, c * n3 : (c + 1) * n3, :] = both[odd * n3 : (odd + 1) * n3]


class Place:
    def __init__(self):
        freq, tile = lax.axis_index("freq"), lax.axis_index("tile")
        self.second = lax.rem(tile, 2) == 1
        self.faces_lower = faces_lower(tile)
        self.has_lower, self.has_upper = freq > 0, freq < lax.axis_size("freq") - 1
        self.has_above, self.has_below = tile > 0, tile < lax.axis_size("tile") - 1


def lane_of(x):
    return lax.broadcasted_iota(jnp.int32, x.shape, 1)


def turned(x, by):
    return pltpu.roll(x, by, 1)


def column_taps(x):
    lane, zero, half = lane_of(x), jnp.zeros_like(x), turned(x, 64)
    before = jnp.where(lane < 64, turned(x, 65), half)
    after = jnp.where(lane < 64, half, turned(x, 63))
    return jnp.where(lane == 0, zero, before), x, jnp.where(lane == 127, zero, after)


def sum_of_taps(before, here, after):
    lane, zero = lane_of(here), jnp.zeros_like(here)
    half = turned(jnp.where(lane < 64, before, after), 64)
    rest = jnp.where(lane < 64, turned(before, 65), turned(after, 63))
    return here + half + jnp.where((lane == 0) | (lane == 127), zero, rest)


def sum_of_even_taps(before, here, after):
    lane, zero = lane_of(here), jnp.zeros_like(here)
    return here + turned(after, 64) + jnp.where(lane == 0, zero, turned(before, 65))


def own_rows(plan, place, ref, plane):
    rows = ref[plane].astype(F32)
    return jnp.where(place.second, rows[plan.strip :], rows[: plan.slots])


def rim_rows(plan, place, ref, plane, inside):
    return jnp.where(inside, own_rows(plan, place, ref, plane), 0.0)


def piece(plan, rows):
    pad = jnp.zeros((plan.plane_k - 3 * plan.slots, 128), F32)
    return jnp.concatenate([*column_taps(rows), pad], axis=0).astype(BF)


def in_twos(planes):
    planes = list(planes)
    return [planes[i : i + 2] for i in range(0, len(planes), 2)]


def layer_one(plan, place, pieces, planes, t1, b1):
    pad = jnp.zeros((plan.k1 - 3 * plan.plane_k, 128), BF)
    strip, made = plan.strip, {}
    for chunk in in_twos(planes):
        x1 = [jnp.concatenate([*pieces[p : p + 3], pad], axis=0) for p in chunk]
        sums = jnp.dot(t1[...], jnp.concatenate(x1, axis=1), preferred_element_type=F32)
        for i, p in enumerate(chunk):
            v = sums[:, i * 128 : (i + 1) * 128].reshape(plan.r1, plan.c1, 128)
            v = leaky_relu(v + b1[...])
            if p < 2:
                v = jnp.where(place.has_lower, v, 0.0)
            if p == plan.planes1 - 1:
                v = jnp.where(place.has_upper, v, 0.0)
            v = jnp.concatenate(
                [
                    jnp.where(place.has_above, v[:2], 0.0),
                    v[2 : strip + 2],
                    jnp.where(place.has_below, v[strip + 2 :], 0.0),
                ],
                axis=0,
            )
            made[p] = v.reshape(plan.n1, 128).astype(BF)
    return made


def blocks_of(planes, rows, step, size, k):
    parts = [plane[step * k : step * k + size] for plane in planes]
    return jnp.concatenate(parts + [jnp.zeros((rows - len(parts) * size, 128), BF)], axis=0)


def layer_two(plan, place, layer_one, planes, t2, b2):
    out2, blocks = plan.out2, {}
    for chunk in in_twos((q, k) for q in planes for k in range(plan.r2 // plan.block2)):
        x = []
        for q, k in chunk:
            x.append(blocks_of([layer_one(q + a) for a in range(3)], plan.k2, out2, plan.in2, k))
        sums = jnp.dot(t2[...], jnp.concatenate(x, axis=1), preferred_element_type=F32)
        for i, (q, k) in enumerate(chunk):
            taps = [sums[c * out2 : (c + 1) * out2, i * 128 : (i + 1) * 128] for c in range(3)]
            v = sum_of_taps(*taps).reshape(plan.block2, plan.c2, 128)
            v = leaky_relu(v + b2[...])
            if q == 0:
                v = jnp.where(place.has_lower, v, 0.0)
            if k == 0:
                v = jnp.concatenate([jnp.where(place.has_above, v[:1], 0.0), v[1:]], axis=0)
            blocks.setdefault(q, []).append(v.reshape(out2, 128).astype(BF))
    return {q: jnp.concatenate(parts, axis=0) for q, parts in blocks.items()}


def layer_three(plan, layer_two, t3, b3, out):
    n3, rows = plan.out3, plan.block3
    for f in range(plan.depth // 2):
        planes = [layer_two(2 * f + a) for a in range(3)]
        for y in range(0, plan.r3, 2 * rows):
            first, second = (
                jnp.dot(
                    t3[odd],
                    blocks_of(planes, plan.k3, 2 * rows * plan.c2, plan.in3, y // rows + odd),
                    preferred_element_type=F32,
                )
                for odd in range(2)
            )
            first, second = (
                sum_of_even_taps(*(half[c * n3 : (c + 1) * n3] for c in range(3))).reshape(
                    plan.c3 // 2, 2 * rows, 128
                )
                for half in (first, second)
            )
            sub = lax.broadcasted_iota(jnp.int32, first.shape, 1)
            one = jnp.where(sub < rows, first, second)
            other = jnp.where(sub < rows, second, first)
            other = jnp.concatenate([other[:, rows:], other[:, :rows]], axis=1)
            v = jnp.stack([one, other], axis=1).reshape(plan.c3, 2 * rows, 128)
            v = leaky_relu(v + b3[:, y : y + 2 * rows])
            out[:, f, y : y + 2 * rows] = v[:, :, :64].astype(BF)


def lower_half(plan, place, own, halo, t1, t2, b1, b2, middle=None):
    pieces = [piece(plan, rim_rows(plan, place, halo, p, place.has_lower)) for p in range(3)]
    pieces += [piece(plan, own_rows(plan, place, own, p)) for p in range(plan.depth if middle is None else 2)]
    made = layer_one(plan, place, pieces, range(plan.depth + 1 if middle is None else 3), t1, b1)
    some = lambda p: made[p] if p in made else middle[p - 3]
    return layer_two(plan, place, some, range(3), t2, b2), made


def upper_half(plan, place, own, halo, t1, t2, b1, b2, middle=None):
    depth = plan.depth
    first = 0 if middle is None else depth - 2
    pieces = [None] * (3 + first)
    pieces += [piece(plan, own_rows(plan, place, own, p)) for p in range(first, depth)]
    pieces += [piece(plan, rim_rows(plan, place, halo, p, place.has_upper)) for p in range(2)]
    made = layer_one(plan, place, pieces, range(3 + first, depth + 3), t1, b1)
    some = lambda p: made[p] if p in made else middle[p - 3]
    return layer_two(plan, place, some, range(3, depth + 1), t2, b2), made


def early_kernel(plan, own, got, t1, t2, b1, b2, done, middle):
    place = Place()

    def run(half):
        planes, made = half(plan, place, own, got, t1, t2, b1, b2)
        for q, v in planes.items():
            done[q] = v
        for p in range(3, plan.depth + 1):
            middle[p - 3] = made[p]

    pl.when(place.faces_lower)(lambda: run(lower_half))
    pl.when(jnp.logical_not(place.faces_lower))(lambda: run(upper_half))


def late_kernel(plan, own, other, middle, done, t1, t2, b1, b2, t3, b3, out):
    place = Place()

    def run(half):
        late, _ = half(plan, place, own, other, t1, t2, b1, b2, middle)
        layer_three(plan, lambda q: late[q] if q in late else done[q], t3, b3, out)

    pl.when(place.faces_lower)(lambda: run(upper_half))
    pl.when(jnp.logical_not(place.faces_lower))(lambda: run(lower_half))


def in_order(upper, held, taken):
    return jnp.where(
        upper,
        jnp.concatenate([taken, held], axis=0),
        jnp.concatenate([held, taken], axis=0),
    )


def chip_rows(plan, planes, chip):
    padded = jnp.pad(planes, ((0, 0), (plan.rim, plan.rim), (0, 0)))
    shape = (planes.shape[0], plan.span, planes.shape[2])
    return lax.dynamic_slice(padded, (0, chip * 2 * plan.strip, 0), shape)


def freq_pairs(groups, tiles, flip):
    pairs = []
    for g in range(groups):
        for t in range(tiles):
            to = g + 1 if t % 2 == 0 else g - 1
            target = (to, t ^ flip) if 0 <= to < groups else (g, (t + 2) % tiles)
            pairs.append((g * tiles + t, target[0] * tiles + target[1]))
    return pairs


def gathered(plan, plane, tiles):
    if tiles & (tiles - 1):
        held = lax.all_gather(plane, "tile", axis=0, tiled=True)
        return chip_rows(plan, held, lax.axis_index("tile") // 2)
    tile, size, held = lax.axis_index("tile"), 1, plane
    while size < tiles:
        taken = lax.ppermute(held, "tile", [(t, t ^ (2 * size - 1)) for t in range(tiles)])
        held = in_order((tile // size) % 2 == 1, held, taken)
        size *= 2
    return chip_rows(plan, held, tile // 2)


def some_planes(planes, tile):
    begin = (jnp.where(faces_lower(tile), planes.shape[0] - 3, 0), 0, 0)
    return lax.dynamic_slice(planes, begin, (3, *planes.shape[1:]))


def even_first(width):
    row = lax.broadcasted_iota(jnp.int32, (width, width), 0)
    col = lax.broadcasted_iota(jnp.int32, (width, width), 1)
    return ones_where(row == 2 * lax.rem(col, width // 2) + lax.div(col, width // 2))


def pair_kernel(plane, taken, pair):
    upper = lax.rem(lax.axis_index("tile"), 2) == 1
    order = even_first(plane.shape[2])
    here, there = (
        jnp.dot(ref[0].astype(BF), order, preferred_element_type=F32).astype(BF) for ref in (plane, taken)
    )
    pair[0] = jnp.where(upper, there, here)
    pair[1] = jnp.where(upper, here, there)


def exchanged(plan, plane, groups, tiles, weights, make_bands):
    axes, tile = ("freq", "tile"), lax.axis_index("tile")
    if tiles != 4:
        planes = jnp.einsum("pyx,xw->pyw", plane.astype(BF), even_first(plane.shape[2]), preferred_element_type=F32)
        own = gathered(plan, planes.astype(BF), tiles)
        message = some_planes(own, tile + 1)
        return own, lax.ppermute(message, axes, freq_pairs(groups, tiles, 1)), make_bands(weights)
    taken = lax.ppermute(plane, "tile", [(t, t ^ 1) for t in range(tiles)])
    pair = pl.pallas_call(
        pair_kernel,
        name="pair",
        out_shape=jax.ShapeDtypeStruct((2, *plane.shape[1:]), BF),
        in_specs=[VM] * 2,
        out_specs=VM,
        compiler_params=pltpu.CompilerParams(vmem_limit_bytes=32 * 2**20),
    )(plane.astype(BF), taken)
    chip = tile // 2
    mine, theirs = chip_rows(plan, pair, chip), chip_rows(plan, pair, 1 - chip)
    ahead = lax.ppermute(mine, axes, freq_pairs(groups, tiles, 1))
    aside = lax.ppermute(theirs, axes, freq_pairs(groups, tiles, 3))
    across = lax.ppermute(theirs, "tile", [(t, t ^ 3) for t in range(tiles)])
    ahead, *weights = lax.optimization_barrier((ahead, *weights))
    bands = make_bands(weights)
    aside, *bands = lax.optimization_barrier((aside, *bands))
    own = in_order(chip == 1, mine, across)
    return own, some_planes(in_order(chip == 1, ahead, aside), tile), bands


def body(sky_cube, kernel_one, bias_one, kernel_two, bias_two, kernel_three, bias_three):
    tiles, groups = lax.axis_size("tile"), lax.axis_size("freq")
    strip = sky_cube.shape[1] // tiles
    depth = tiles * sky_cube.shape[0]
    c1, c2, c3 = (kernel.shape[0] for kernel in (kernel_one, kernel_two, kernel_three))
    plan = Plan(strip, depth, c1, c2, c3)
    tile = lax.axis_index("tile")

    w1 = jnp.transpose(kernel_one[:, 0], (1, 2, 3, 0))
    w2 = jnp.transpose(kernel_two, (2, 3, 4, 0, 1))
    w3 = jnp.transpose(kernel_three, (2, 3, 4, 1, 0))

    params = pltpu.CompilerParams(vmem_limit_bytes=32 * 2**20)

    def make_bands(weights):
        return pl.pallas_call(
            functools.partial(bands_kernel, plan),
            name="bands",
            out_shape=[
                jax.ShapeDtypeStruct((plan.n1, plan.k1), BF),
                jax.ShapeDtypeStruct((3 * plan.out2, plan.k2), BF),
                jax.ShapeDtypeStruct((c1, 128), F32),
                jax.ShapeDtypeStruct((c2, 128), F32),
                jax.ShapeDtypeStruct((c3, plan.r3, 128), F32),
                jax.ShapeDtypeStruct((2, 3 * plan.out3, plan.k3), BF),
            ],
            in_specs=[VM] * 6,
            out_specs=[VM] * 6,
            compiler_params=params,
        )(*weights)

    own, got, weights = exchanged(
        plan, sky_cube, groups, tiles, (bias_one[None], bias_two[None], bias_three[None], w1, w2, w3), make_bands
    )
    t1, t2, b1, b2, b3, t3 = weights
    other = lax.ppermute(got, "tile", [(t, t ^ 1) for t in range(tiles)])
    done, middle = pl.pallas_call(
        functools.partial(early_kernel, plan),
        name="early",
        out_shape=[
            jax.ShapeDtypeStruct((plan.planes2, plan.n2, 128), BF),
            jax.ShapeDtypeStruct((depth - 2, plan.n1, 128), BF),
        ],
        in_specs=[VM] * 6,
        out_specs=[VM] * 2,
        compiler_params=params,
    )(own, got, t1, t2, b1, b2)
    other, done = lax.optimization_barrier((other, done))
    return pl.pallas_call(
        functools.partial(late_kernel, plan),
        name="late",
        out_shape=jax.ShapeDtypeStruct((c3, depth // 2, plan.r3, sky_cube.shape[2] // 2), BF),
        in_specs=[VM] * 10,
        out_specs=VM,
        compiler_params=params,
    )(own, other, middle, done, t1, t2, b1, b2, t3, b3)


def solution(mesh):
    return jax.shard_map(
        body,
        mesh=mesh,
        in_specs=(P(("freq", "tile"), None, None), P(), P(), P(), P(), P(), P()),
        out_specs=P(None, "freq", "tile", None),
        check_vma=False,
    )
```

```python
import functools

import jax
import jax.numpy as jnp
from jax import lax
from jax.experimental import pallas as pl
from jax.experimental.pallas import tpu as pltpu
from jax.sharding import PartitionSpec as P

BF = jnp.bfloat16
F32 = jnp.float32
VM = pl.BlockSpec(memory_space=pltpu.VMEM)


def even(n):
    return n + n % 2


def up_to(n, unit):
    return -(-n // unit) * unit


class Plan:
    def __init__(self, strip, depth, c1, c2, c3):
        self.strip, self.depth, self.c1, self.c2, self.c3 = strip, depth, c1, c2, c3
        self.rim = 4
        self.slots = strip + 2 * self.rim
        self.span = 2 * strip + 2 * self.rim
        self.plane_k = up_to(3 * self.slots, 16)
        self.k1 = up_to(3 * self.plane_k, 256)
        self.block2, self.block3 = 6, 4
        self.r2 = up_to(strip + 1, self.block2)
        self.r1 = self.r2 + 2
        self.r3 = strip // 2
        self.n1, self.n2 = self.r1 * c1, self.r2 * c2
        self.in2, self.out2 = (self.block2 + 2) * c1, self.block2 * c2
        self.in3, self.out3 = (2 * self.block3 + 2) * c2, self.block3 * c3
        self.k2, self.k3 = up_to(3 * self.in2, 256), up_to(3 * self.in3, 256)
        self.planes1, self.planes2 = depth + 3, depth + 1


def leaky_relu(values):
    return jnp.maximum(values, 0.1 * values)


def faces_lower(tile):
    return tile % 2 == 1


def column_of(bias_ref, rows):
    at = lax.broadcasted_iota(jnp.int32, (rows, rows), 0)
    lane = lax.broadcasted_iota(jnp.int32, (rows, rows), 1)
    spread = jnp.where(at == lane, jnp.broadcast_to(bias_ref[...], (rows, rows)), 0.0)
    return jnp.broadcast_to(jnp.sum(spread, axis=1, keepdims=True), (rows, 128))


def ones_where(hit):
    return hit.astype(F32).astype(BF)


def dot_over_rows(left, right):
    return lax.dot_general(left, right, (((0,), (0,)), ((), ())), preferred_element_type=F32)


def rolled(x, by):
    return pltpu.roll(x, by, 1) if by else x


def bands_kernel(plan, bias1, bias2, bias3, w1, w2, w3, t1, t2, b1, b2, b3, t3):
    c1, c2 = plan.c1, plan.c2
    slots = plan.slots
    bands_3(plan, w3, t3)
    b1[...] = column_of(bias1, c1)
    b2[...] = column_of(bias2, c2)
    column = column_of(bias3, plan.c3)
    b3[...] = jnp.broadcast_to(column[:, None], b3.shape)
    tap = lax.broadcasted_iota(jnp.int32, (3, plan.k1), 0)
    lane = lax.broadcasted_iota(jnp.int32, (3, plan.k1), 1)
    taps = []
    for b in range(3):
        taps.append(
            sum(
                dot_over_rows(w1[a, b], ones_where(lane == a * plan.plane_k + tap * slots))
                for a in range(3)
            )
        )
    base = sum(rolled(taps[b], b) for b in range(3))
    for y in range(0, plan.r1, 2):
        rows = [rolled(base, y + k + plan.rim - 3) for k in range(2)]
        t1[y * c1 : (y + 2) * c1, :] = jnp.concatenate(rows, axis=0).astype(BF)

    for c in range(3):
        parts = [jnp.zeros((c2, 128), F32) for _ in range(plan.k2 // 128)]
        for a in range(3):
            for b in range(3):
                at = a * plan.in2 + b * c1
                tile = w2[a, b, c].astype(F32)
                tile = jnp.concatenate([tile, jnp.zeros((c2, 128 - c1), F32)], axis=1)
                parts[at // 128] += rolled(tile, at % 128)
        base = jnp.concatenate(parts, axis=1)
        for y in range(0, plan.block2, 2):
            rows = [rolled(base, (y + k) * c1) for k in range(2)]
            at = c * plan.out2 + y * c2
            t2[at : at + 2 * c2, :] = jnp.concatenate(rows, axis=0).astype(BF)


def parts_of(count, *sizes):
    at, digits = lax.broadcasted_iota(jnp.int32, (count, 1), 0), []
    for size in reversed(sizes):
        digits.append(lax.rem(at, size))
        at = lax.div(at, size)
    return at, *reversed(digits)


def bands_3(plan, w3, t3):
    c2, c3, rows = plan.c2, plan.c3, plan.block3
    n3 = plan.out3
    odd, pair, which, y = parts_of(2 * n3, c3 // 2, 2, rows)
    source = lax.broadcasted_iota(jnp.int32, (2 * n3, n3), 1)
    turn = ones_where(source == y * c3 + 2 * pair + lax.rem(which + odd, 2))
    a, b, i = parts_of(9 * c2, 3, c2)
    lane = lax.broadcasted_iota(jnp.int32, (9 * c2, plan.k3), 1)
    spread = ones_where(lane == a * plan.in3 + b * c2 + i)
    for c in range(3):
        taken = w3[:, :, c].astype(F32).reshape(9 * c2, c3).astype(BF)
        base = dot_over_rows(taken, spread)
        stacked = [rolled(base, 2 * y * c2) for y in range(rows)]
        stacked = jnp.concatenate(stacked, axis=0).astype(BF)
        both = jnp.dot(turn, stacked, preferred_element_type=F32).astype(BF)
        for odd in range(2):
            t3[odd, c * n3 : (c + 1) * n3, :] = both[odd * n3 : (odd + 1) * n3]


class Place:
    def __init__(self):
        freq, tile = lax.axis_index("freq"), lax.axis_index("tile")
        self.second = lax.rem(tile, 2) == 1
        self.faces_lower = faces_lower(tile)
        self.has_lower, self.has_upper = freq > 0, freq < lax.axis_size("freq") - 1
        self.has_above, self.has_below = tile > 0, tile < lax.axis_size("tile") - 1


def lane_of(x):
    return lax.broadcasted_iota(jnp.int32, x.shape, 1)


def turned(x, by):
    return pltpu.roll(x, by, 1)


def column_taps(x):
    lane, zero, half = lane_of(x), jnp.zeros_like(x), turned(x, 64)
    before = jnp.where(lane < 64, turned(x, 65), half)
    after = jnp.where(lane < 64, half, turned(x, 63))
    return jnp.where(lane == 0, zero, before), x, jnp.where(lane == 127, zero, after)


def sum_of_taps(before, here, after):
    lane, zero = lane_of(here), jnp.zeros_like(here)
    half = turned(jnp.where(lane < 64, before, after), 64)
    rest = jnp.where(lane < 64, turned(before, 65), turned(after, 63))
    return here + half + jnp.where((lane == 0) | (lane == 127), zero, rest)


def sum_of_even_taps(before, here, after):
    lane, zero = lane_of(here), jnp.zeros_like(here)
    return here + turned(after, 64) + jnp.where(lane == 0, zero, turned(before, 65))


def own_rows(plan, place, ref, plane):
    rows = ref[plane].astype(F32)
    return jnp.where(place.second, rows[plan.strip :], rows[: plan.slots])


def rim_rows(plan, place, ref, plane, inside):
    return jnp.where(inside, own_rows(plan, place, ref, plane), 0.0)


def piece(plan, rows):
    pad = jnp.zeros((plan.plane_k - 3 * plan.slots, 128), F32)
    return jnp.concatenate([*column_taps(rows), pad], axis=0).astype(BF)


def in_twos(planes):
    planes = list(planes)
    return [planes[i : i + 2] for i in range(0, len(planes), 2)]


def layer_one(plan, place, pieces, planes, t1, b1):
    pad = jnp.zeros((plan.k1 - 3 * plan.plane_k, 128), BF)
    strip, made = plan.strip, {}
    for chunk in in_twos(planes):
        x1 = [jnp.concatenate([*pieces[p : p + 3], pad], axis=0) for p in chunk]
        sums = jnp.dot(t1[...], jnp.concatenate(x1, axis=1), preferred_element_type=F32)
        for i, p in enumerate(chunk):
            v = sums[:, i * 128 : (i + 1) * 128].reshape(plan.r1, plan.c1, 128)
            v = leaky_relu(v + b1[...])
            if p < 2:
                v = jnp.where(place.has_lower, v, 0.0)
            if p == plan.planes1 - 1:
                v = jnp.where(place.has_upper, v, 0.0)
            v = jnp.concatenate(
                [
                    jnp.where(place.has_above, v[:2], 0.0),
                    v[2 : strip + 2],
                    jnp.where(place.has_below, v[strip + 2 :], 0.0),
                ],
                axis=0,
            )
            made[p] = v.reshape(plan.n1, 128).astype(BF)
    return made


def blocks_of(planes, rows, step, size, k):
    parts = [plane[step * k : step * k + size] for plane in planes]
    return jnp.concatenate(parts + [jnp.zeros((rows - len(parts) * size, 128), BF)], axis=0)


def layer_two(plan, place, layer_one, planes, t2, b2):
    out2, blocks = plan.out2, {}
    for chunk in in_twos((q, k) for q in planes for k in range(plan.r2 // plan.block2)):
        x = []
        for q, k in chunk:
            x.append(blocks_of([layer_one(q + a) for a in range(3)], plan.k2, out2, plan.in2, k))
        sums = jnp.dot(t2[...], jnp.concatenate(x, axis=1), preferred_element_type=F32)
        for i, (q, k) in enumerate(chunk):
            taps = [sums[c * out2 : (c + 1) * out2, i * 128 : (i + 1) * 128] for c in range(3)]
            v = sum_of_taps(*taps).reshape(plan.block2, plan.c2, 128)
            v = leaky_relu(v + b2[...])
            if q == 0:
                v = jnp.where(place.has_lower, v, 0.0)
            if k == 0:
                v = jnp.concatenate([jnp.where(place.has_above, v[:1], 0.0), v[1:]], axis=0)
            blocks.setdefault(q, []).append(v.reshape(out2, 128).astype(BF))
    return {q: jnp.concatenate(parts, axis=0) for q, parts in blocks.items()}


def layer_three(plan, layer_two, t3, b3, out):
    n3, rows = plan.out3, plan.block3
    for f in range(plan.depth // 2):
        planes = [layer_two(2 * f + a) for a in range(3)]
        for y in range(0, plan.r3, 2 * rows):
            first, second = (
                jnp.dot(
                    t3[odd],
                    blocks_of(planes, plan.k3, 2 * rows * plan.c2, plan.in3, y // rows + odd),
                    preferred_element_type=F32,
                )
                for odd in range(2)
            )
            first, second = (
                sum_of_even_taps(*(half[c * n3 : (c + 1) * n3] for c in range(3))).reshape(
                    plan.c3 // 2, 2 * rows, 128
                )
                for half in (first, second)
            )
            sub = lax.broadcasted_iota(jnp.int32, first.shape, 1)
            one = jnp.where(sub < rows, first, second)
            other = jnp.where(sub < rows, second, first)
            other = jnp.concatenate([other[:, rows:], other[:, :rows]], axis=1)
            v = jnp.stack([one, other], axis=1).reshape(plan.c3, 2 * rows, 128)
            v = leaky_relu(v + b3[:, y : y + 2 * rows])
            out[:, f, y : y + 2 * rows] = v[:, :, :64].astype(BF)


def lower_half(plan, place, own, halo, t1, t2, b1, b2, middle=None):
    pieces = [piece(plan, rim_rows(plan, place, halo, p, place.has_lower)) for p in range(3)]
    pieces += [piece(plan, own_rows(plan, place, own, p)) for p in range(plan.depth if middle is None else 2)]
    made = layer_one(plan, place, pieces, range(plan.depth + 1 if middle is None else 3), t1, b1)
    some = lambda p: made[p] if p in made else middle[p - 3]
    return layer_two(plan, place, some, range(3), t2, b2), made


def upper_half(plan, place, own, halo, t1, t2, b1, b2, middle=None):
    depth = plan.depth
    first = 0 if middle is None else depth - 2
    pieces = [None] * (3 + first)
    pieces += [piece(plan, own_rows(plan, place, own, p)) for p in range(first, depth)]
    pieces += [piece(plan, rim_rows(plan, place, halo, p, place.has_upper)) for p in range(2)]
    made = layer_one(plan, place, pieces, range(3 + first, depth + 3), t1, b1)
    some = lambda p: made[p] if p in made else middle[p - 3]
    return layer_two(plan, place, some, range(3, depth + 1), t2, b2), made


def early_kernel(plan, own, got, t1, t2, b1, b2, done, middle):
    place = Place()

    def run(half):
        planes, made = half(plan, place, own, got, t1, t2, b1, b2)
        for q, v in planes.items():
            done[q] = v
        for p in range(3, plan.depth + 1):
            middle[p - 3] = made[p]

    pl.when(place.faces_lower)(lambda: run(lower_half))
    pl.when(jnp.logical_not(place.faces_lower))(lambda: run(upper_half))


def late_kernel(plan, own, other, middle, done, t1, t2, b1, b2, t3, b3, out):
    place = Place()

    def run(half):
        late, _ = half(plan, place, own, other, t1, t2, b1, b2, middle)
        layer_three(plan, lambda q: late[q] if q in late else done[q], t3, b3, out)

    pl.when(place.faces_lower)(lambda: run(upper_half))
    pl.when(jnp.logical_not(place.faces_lower))(lambda: run(lower_half))


def in_order(upper, held, taken):
    return jnp.where(
        upper,
        jnp.concatenate([taken, held], axis=0),
        jnp.concatenate([held, taken], axis=0),
    )


def chip_rows(plan, planes, chip):
    padded = jnp.pad(planes, ((0, 0), (plan.rim, plan.rim), (0, 0)))
    shape = (planes.shape[0], plan.span, planes.shape[2])
    return lax.dynamic_slice(padded, (0, chip * 2 * plan.strip, 0), shape)


def freq_pairs(groups, tiles, flip):
    pairs = []
    for g in range(groups):
        for t in range(tiles):
            to = g + 1 if t % 2 == 0 else g - 1
            target = (to, t ^ flip) if 0 <= to < groups else (g, (t + 2) % tiles)
            pairs.append((g * tiles + t, target[0] * tiles + target[1]))
    return pairs


def gathered(plan, plane, tiles):
    if tiles & (tiles - 1):
        held = lax.all_gather(plane, "tile", axis=0, tiled=True)
        return chip_rows(plan, held, lax.axis_index("tile") // 2)
    tile, size, held = lax.axis_index("tile"), 1, plane
    while size < tiles:
        taken = lax.ppermute(held, "tile", [(t, t ^ (2 * size - 1)) for t in range(tiles)])
        held = in_order((tile // size) % 2 == 1, held, taken)
        size *= 2
    return chip_rows(plan, held, tile // 2)


def some_planes(planes, tile):
    begin = (jnp.where(faces_lower(tile), planes.shape[0] - 3, 0), 0, 0)
    return lax.dynamic_slice(planes, begin, (3, *planes.shape[1:]))


def even_first(width):
    row = lax.broadcasted_iota(jnp.int32, (width, width), 0)
    col = lax.broadcasted_iota(jnp.int32, (width, width), 1)
    return ones_where(row == 2 * lax.rem(col, width // 2) + lax.div(col, width // 2))


def pair_kernel(plan, plane, taken, mine, theirs):
    tile = lax.axis_index("tile")
    upper, second = lax.rem(tile, 2) == 1, tile >= 2
    order = even_first(plane.shape[2])
    inside = plan.span - plan.rim
    edge = jnp.zeros((plan.rim, plane.shape[2]), F32)
    here, there = (jnp.dot(ref[0].astype(BF), order, preferred_element_type=F32) for ref in (plane, taken))
    for p, rows in enumerate((jnp.where(upper, there, here), jnp.where(upper, here, there))):
        top = jnp.concatenate([edge, rows[:inside]], axis=0)
        bottom = jnp.concatenate([rows[rows.shape[0] - inside :], edge], axis=0)
        mine[p] = jnp.where(second, bottom, top).astype(BF)
        theirs[p] = jnp.where(second, top, bottom).astype(BF)


def exchanged(plan, plane, groups, tiles, weights, make_bands):
    axes, tile = ("freq", "tile"), lax.axis_index("tile")
    if tiles != 4:
        planes = jnp.einsum("pyx,xw->pyw", plane.astype(BF), even_first(plane.shape[2]), preferred_element_type=F32)
        own = gathered(plan, planes.astype(BF), tiles)
        message = some_planes(own, tile + 1)
        return own, lax.ppermute(message, axes, freq_pairs(groups, tiles, 1)), make_bands(weights)
    taken = lax.ppermute(plane, "tile", [(t, t ^ 1) for t in range(tiles)])
    window = jax.ShapeDtypeStruct((2, plan.span, plane.shape[2]), BF)
    mine, theirs = pl.pallas_call(
        functools.partial(pair_kernel, plan),
        name="pair",
        out_shape=[window] * 2,
        in_specs=[VM] * 2,
        out_specs=[VM] * 2,
        compiler_params=pltpu.CompilerParams(vmem_limit_bytes=32 * 2**20),
    )(plane.astype(BF), taken)
    chip = tile // 2
    ahead = lax.ppermute(mine, axes, freq_pairs(groups, tiles, 1))
    aside = lax.ppermute(theirs, axes, freq_pairs(groups, tiles, 3))
    across = lax.ppermute(theirs, "tile", [(t, t ^ 3) for t in range(tiles)])
    ahead, *weights = lax.optimization_barrier((ahead, *weights))
    bands = make_bands(weights)
    aside, *bands = lax.optimization_barrier((aside, *bands))
    own = in_order(chip == 1, mine, across)
    return own, some_planes(in_order(chip == 1, ahead, aside), tile), bands


def body(sky_cube, kernel_one, bias_one, kernel_two, bias_two, kernel_three, bias_three):
    tiles, groups = lax.axis_size("tile"), lax.axis_size("freq")
    strip = sky_cube.shape[1] // tiles
    depth = tiles * sky_cube.shape[0]
    c1, c2, c3 = (kernel.shape[0] for kernel in (kernel_one, kernel_two, kernel_three))
    plan = Plan(strip, depth, c1, c2, c3)
    tile = lax.axis_index("tile")

    w1 = jnp.transpose(kernel_one[:, 0], (1, 2, 3, 0))
    w2 = jnp.transpose(kernel_two, (2, 3, 4, 0, 1))
    w3 = jnp.transpose(kernel_three, (2, 3, 4, 1, 0))

    params = pltpu.CompilerParams(vmem_limit_bytes=32 * 2**20)

    def make_bands(weights):
        return pl.pallas_call(
            functools.partial(bands_kernel, plan),
            name="bands",
            out_shape=[
                jax.ShapeDtypeStruct((plan.n1, plan.k1), BF),
                jax.ShapeDtypeStruct((3 * plan.out2, plan.k2), BF),
                jax.ShapeDtypeStruct((c1, 128), F32),
                jax.ShapeDtypeStruct((c2, 128), F32),
                jax.ShapeDtypeStruct((c3, plan.r3, 128), F32),
                jax.ShapeDtypeStruct((2, 3 * plan.out3, plan.k3), BF),
            ],
            in_specs=[VM] * 6,
            out_specs=[VM] * 6,
            compiler_params=params,
        )(*weights)

    own, got, weights = exchanged(
        plan, sky_cube, groups, tiles, (bias_one[None], bias_two[None], bias_three[None], w1, w2, w3), make_bands
    )
    t1, t2, b1, b2, b3, t3 = weights
    other = lax.ppermute(got, "tile", [(t, t ^ 1) for t in range(tiles)])
    done, middle = pl.pallas_call(
        functools.partial(early_kernel, plan),
        name="early",
        out_shape=[
            jax.ShapeDtypeStruct((plan.planes2, plan.n2, 128), BF),
            jax.ShapeDtypeStruct((depth - 2, plan.n1, 128), BF),
        ],
        in_specs=[VM] * 6,
        out_specs=[VM] * 2,
        compiler_params=params,
    )(own, got, t1, t2, b1, b2)
    other, done = lax.optimization_barrier((other, done))
    return pl.pallas_call(
        functools.partial(late_kernel, plan),
        name="late",
        out_shape=jax.ShapeDtypeStruct((c3, depth // 2, plan.r3, sky_cube.shape[2] // 2), BF),
        in_specs=[VM] * 10,
        out_specs=VM,
        compiler_params=params,
    )(own, other, middle, done, t1, t2, b1, b2, t3, b3)


def solution(mesh):
    return jax.shard_map(
        body,
        mesh=mesh,
        in_specs=(P(("freq", "tile"), None, None), P(), P(), P(), P(), P(), P()),
        out_specs=P(None, "freq", "tile", None),
        check_vma=False,
    )
```

```python
import functools

import jax
import jax.numpy as jnp
from jax import lax
from jax.experimental import pallas as pl
from jax.experimental.pallas import tpu as pltpu
from jax.sharding import PartitionSpec as P

BF = jnp.bfloat16
F32 = jnp.float32
VM = pl.BlockSpec(memory_space=pltpu.VMEM)


def even(n):
    return n + n % 2


def up_to(n, unit):
    return -(-n // unit) * unit


class Plan:
    def __init__(self, strip, depth, c1, c2, c3):
        self.strip, self.depth, self.c1, self.c2, self.c3 = strip, depth, c1, c2, c3
        self.rim = 4
        self.slots = strip + 2 * self.rim
        self.span = 2 * strip + 2 * self.rim
        self.plane_k = up_to(3 * self.slots, 16)
        self.k1 = up_to(3 * self.plane_k, 256)
        self.block2, self.block3 = 6, 4
        self.r2 = up_to(strip + 1, self.block2)
        self.r1 = self.r2 + 2
        self.r3 = strip // 2
        self.n1, self.n2 = self.r1 * c1, self.r2 * c2
        self.in2, self.out2 = (self.block2 + 2) * c1, self.block2 * c2
        self.in3, self.out3 = (2 * self.block3 + 2) * c2, self.block3 * c3
        self.k2, self.k3 = up_to(3 * self.in2, 256), up_to(3 * self.in3, 256)
        self.planes1, self.planes2 = depth + 3, depth + 1


def leaky_relu(values):
    return jnp.maximum(values, 0.1 * values)


def faces_lower(tile):
    return tile % 2 == 1


def column_of(bias_ref, rows):
    at = lax.broadcasted_iota(jnp.int32, (rows, rows), 0)
    lane = lax.broadcasted_iota(jnp.int32, (rows, rows), 1)
    spread = jnp.where(at == lane, jnp.broadcast_to(bias_ref[...], (rows, rows)), 0.0)
    return jnp.broadcast_to(jnp.sum(spread, axis=1, keepdims=True), (rows, 128))


def ones_where(hit):
    return hit.astype(F32).astype(BF)


def dot_over_rows(left, right):
    return lax.dot_general(left, right, (((0,), (0,)), ((), ())), preferred_element_type=F32)


def rolled(x, by):
    return pltpu.roll(x, by, 1) if by else x


def bands_kernel(plan, bias1, bias2, bias3, w1, w2, w3, t1, t2, b1, b2, b3, t3):
    c1, c2 = plan.c1, plan.c2
    slots = plan.slots
    bands_3(plan, w3, t3)
    b1[...] = column_of(bias1, c1)
    b2[...] = column_of(bias2, c2)
    column = column_of(bias3, plan.c3)
    b3[...] = jnp.broadcast_to(column[:, None], b3.shape)
    tap = lax.broadcasted_iota(jnp.int32, (3, plan.k1), 0)
    lane = lax.broadcasted_iota(jnp.int32, (3, plan.k1), 1)
    taps = []
    for b in range(3):
        taps.append(
            sum(
                dot_over_rows(w1[a, b], ones_where(lane == a * plan.plane_k + tap * slots))
                for a in range(3)
            )
        )
    base = sum(rolled(taps[b], b) for b in range(3))
    for y in range(0, plan.r1, 2):
        rows = [rolled(base, y + k + plan.rim - 3) for k in range(2)]
        t1[y * c1 : (y + 2) * c1, :] = jnp.concatenate(rows, axis=0).astype(BF)

    for c in range(3):
        parts = [jnp.zeros((c2, 128), F32) for _ in range(plan.k2 // 128)]
        for a in range(3):
            for b in range(3):
                at = a * plan.in2 + b * c1
                tile = w2[a, b, c].astype(F32)
                tile = jnp.concatenate([tile, jnp.zeros((c2, 128 - c1), F32)], axis=1)
                parts[at // 128] += rolled(tile, at % 128)
        base = jnp.concatenate(parts, axis=1)
        for y in range(0, plan.block2, 2):
            rows = [rolled(base, (y + k) * c1) for k in range(2)]
            at = c * plan.out2 + y * c2
            t2[at : at + 2 * c2, :] = jnp.concatenate(rows, axis=0).astype(BF)


def parts_of(count, *sizes):
    at, digits = lax.broadcasted_iota(jnp.int32, (count, 1), 0), []
    for size in reversed(sizes):
        digits.append(lax.rem(at, size))
        at = lax.div(at, size)
    return at, *reversed(digits)


def bands_3(plan, w3, t3):
    c2, c3, rows = plan.c2, plan.c3, plan.block3
    n3 = plan.out3
    odd, pair, which, y = parts_of(2 * n3, c3 // 2, 2, rows)
    source = lax.broadcasted_iota(jnp.int32, (2 * n3, n3), 1)
    turn = ones_where(source == y * c3 + 2 * pair + lax.rem(which + odd, 2))
    a, b, i = parts_of(9 * c2, 3, c2)
    lane = lax.broadcasted_iota(jnp.int32, (9 * c2, plan.k3), 1)
    spread = ones_where(lane == a * plan.in3 + b * c2 + i)
    for c in range(3):
        taken = w3[:, :, c].astype(F32).reshape(9 * c2, c3).astype(BF)
        base = dot_over_rows(taken, spread)
        stacked = [rolled(base, 2 * y * c2) for y in range(rows)]
        stacked = jnp.concatenate(stacked, axis=0).astype(BF)
        both = jnp.dot(turn, stacked, preferred_element_type=F32).astype(BF)
        for odd in range(2):
            t3[odd, c * n3 : (c + 1) * n3, :] = both[odd * n3 : (odd + 1) * n3]


class Place:
    def __init__(self):
        freq, tile = lax.axis_index("freq"), lax.axis_index("tile")
        self.second = lax.rem(tile, 2) == 1
        self.faces_lower = faces_lower(tile)
        self.has_lower, self.has_upper = freq > 0, freq < lax.axis_size("freq") - 1
        self.has_above, self.has_below = tile > 0, tile < lax.axis_size("tile") - 1


def lane_of(x):
    return lax.broadcasted_iota(jnp.int32, x.shape, 1)


def turned(x, by):
    return pltpu.roll(x, by, 1)


def column_taps(x):
    lane, zero, half = lane_of(x), jnp.zeros_like(x), turned(x, 64)
    before = jnp.where(lane < 64, turned(x, 65), half)
    after = jnp.where(lane < 64, half, turned(x, 63))
    return jnp.where(lane == 0, zero, before), x, jnp.where(lane == 127, zero, after)


def sum_of_taps(before, here, after):
    lane, zero = lane_of(here), jnp.zeros_like(here)
    half = turned(jnp.where(lane < 64, before, after), 64)
    rest = jnp.where(lane < 64, turned(before, 65), turned(after, 63))
    return here + half + jnp.where((lane == 0) | (lane == 127), zero, rest)


def sum_of_even_taps(before, here, after):
    lane, zero = lane_of(here), jnp.zeros_like(here)
    return here + turned(after, 64) + jnp.where(lane == 0, zero, turned(before, 65))


def own_rows(plan, place, ref, plane):
    rows = ref[plane].astype(F32)
    return jnp.where(place.second, rows[plan.strip :], rows[: plan.slots])


def rim_rows(plan, place, ref, plane, inside):
    return jnp.where(inside, own_rows(plan, place, ref, plane), 0.0)


def piece(plan, rows):
    pad = jnp.zeros((plan.plane_k - 3 * plan.slots, 128), F32)
    return jnp.concatenate([*column_taps(rows), pad], axis=0).astype(BF)


def in_twos(planes):
    planes = list(planes)
    return [planes[i : i + 2] for i in range(0, len(planes), 2)]


def layer_one(plan, place, pieces, planes, t1, b1):
    pad = jnp.zeros((plan.k1 - 3 * plan.plane_k, 128), BF)
    strip, made = plan.strip, {}
    for chunk in in_twos(planes):
        x1 = [jnp.concatenate([*pieces[p : p + 3], pad], axis=0) for p in chunk]
        sums = jnp.dot(t1[...], jnp.concatenate(x1, axis=1), preferred_element_type=F32)
        for i, p in enumerate(chunk):
            v = sums[:, i * 128 : (i + 1) * 128].reshape(plan.r1, plan.c1, 128)
            v = leaky_relu(v + b1[...])
            if p < 2:
                v = jnp.where(place.has_lower, v, 0.0)
            if p == plan.planes1 - 1:
                v = jnp.where(place.has_upper, v, 0.0)
            v = jnp.concatenate(
                [
                    jnp.where(place.has_above, v[:2], 0.0),
                    v[2 : strip + 2],
                    jnp.where(place.has_below, v[strip + 2 :], 0.0),
                ],
                axis=0,
            )
            made[p] = v.reshape(plan.n1, 128).astype(BF)
    return made


def blocks_of(planes, rows, step, size, k):
    parts = [plane[step * k : step * k + size] for plane in planes]
    return jnp.concatenate(parts + [jnp.zeros((rows - len(parts) * size, 128), BF)], axis=0)


def layer_two(plan, place, layer_one, planes, t2, b2):
    out2, blocks = plan.out2, {}
    for chunk in in_twos((q, k) for q in planes for k in range(plan.r2 // plan.block2)):
        x = []
        for q, k in chunk:
            x.append(blocks_of([layer_one(q + a) for a in range(3)], plan.k2, out2, plan.in2, k))
        sums = jnp.dot(t2[...], jnp.concatenate(x, axis=1), preferred_element_type=F32)
        for i, (q, k) in enumerate(chunk):
            taps = [sums[c * out2 : (c + 1) * out2, i * 128 : (i + 1) * 128] for c in range(3)]
            v = sum_of_taps(*taps).reshape(plan.block2, plan.c2, 128)
            v = leaky_relu(v + b2[...])
            if q == 0:
                v = jnp.where(place.has_lower, v, 0.0)
            if k == 0:
                v = jnp.concatenate([jnp.where(place.has_above, v[:1], 0.0), v[1:]], axis=0)
            blocks.setdefault(q, []).append(v.reshape(out2, 128).astype(BF))
    return {q: jnp.concatenate(parts, axis=0) for q, parts in blocks.items()}


def layer_three(plan, layer_two, t3, b3, out, order):
    n3, rows = plan.out3, plan.block3
    for f in order:
        planes = [layer_two(2 * f + a) for a in range(3)]
        for y in range(0, plan.r3, 2 * rows):
            first, second = (
                jnp.dot(
                    t3[odd],
                    blocks_of(planes, plan.k3, 2 * rows * plan.c2, plan.in3, y // rows + odd),
                    preferred_element_type=F32,
                )
                for odd in range(2)
            )
            first, second = (
                sum_of_even_taps(*(half[c * n3 : (c + 1) * n3] for c in range(3))).reshape(
                    plan.c3 // 2, 2 * rows, 128
                )
                for half in (first, second)
            )
            sub = lax.broadcasted_iota(jnp.int32, first.shape, 1)
            one = jnp.where(sub < rows, first, second)
            other = jnp.where(sub < rows, second, first)
            other = jnp.concatenate([other[:, rows:], other[:, :rows]], axis=1)
            v = jnp.stack([one, other], axis=1).reshape(plan.c3, 2 * rows, 128)
            v = leaky_relu(v + b3[:, y : y + 2 * rows])
            out[:, f, y : y + 2 * rows] = v[:, :, :64].astype(BF)


def lower_half(plan, place, own, halo, t1, t2, b1, b2, middle=None):
    pieces = [piece(plan, rim_rows(plan, place, halo, p, place.has_lower)) for p in range(3)]
    pieces += [piece(plan, own_rows(plan, place, own, p)) for p in range(plan.depth if middle is None else 2)]
    made = layer_one(plan, place, pieces, range(plan.depth + 1) if middle is None else (2, 1, 0), t1, b1)
    some = lambda p: made[p] if p in made else middle[p - 3]
    return layer_two(plan, place, some, (2, 1, 0), t2, b2), made


def upper_half(plan, place, own, halo, t1, t2, b1, b2, middle=None):
    depth = plan.depth
    first = 0 if middle is None else depth - 2
    pieces = [None] * (3 + first)
    pieces += [piece(plan, own_rows(plan, place, own, p)) for p in range(first, depth)]
    pieces += [piece(plan, rim_rows(plan, place, halo, p, place.has_upper)) for p in range(2)]
    made = layer_one(plan, place, pieces, range(3 + first, depth + 3), t1, b1)
    some = lambda p: made[p] if p in made else middle[p - 3]
    return layer_two(plan, place, some, range(3, depth + 1), t2, b2), made


def early_kernel(plan, own, got, t1, t2, b1, b2, done, middle):
    place = Place()

    def run(half):
        planes, made = half(plan, place, own, got, t1, t2, b1, b2)
        for q, v in planes.items():
            done[q] = v
        for p in range(3, plan.depth + 1):
            middle[p - 3] = made[p]

    pl.when(place.faces_lower)(lambda: run(lower_half))
    pl.when(jnp.logical_not(place.faces_lower))(lambda: run(upper_half))


def late_kernel(plan, own, other, middle, done, t1, t2, b1, b2, t3, b3, out):
    place = Place()

    def run(half, order):
        late, _ = half(plan, place, own, other, t1, t2, b1, b2, middle)
        layer_three(plan, lambda q: late[q] if q in late else done[q], t3, b3, out, order)

    first = range(plan.depth // 2)
    pl.when(place.faces_lower)(lambda: run(upper_half, first))
    pl.when(jnp.logical_not(place.faces_lower))(lambda: run(lower_half, first[::-1]))


def in_order(upper, held, taken):
    return jnp.where(
        upper,
        jnp.concatenate([taken, held], axis=0),
        jnp.concatenate([held, taken], axis=0),
    )


def chip_rows(plan, planes, chip):
    padded = jnp.pad(planes, ((0, 0), (plan.rim, plan.rim), (0, 0)))
    shape = (planes.shape[0], plan.span, planes.shape[2])
    return lax.dynamic_slice(padded, (0, chip * 2 * plan.strip, 0), shape)


def freq_pairs(groups, tiles, flip):
    pairs = []
    for g in range(groups):
        for t in range(tiles):
            to = g + 1 if t % 2 == 0 else g - 1
            target = (to, t ^ flip) if 0 <= to < groups else (g, (t + 2) % tiles)
            pairs.append((g * tiles + t, target[0] * tiles + target[1]))
    return pairs


def gathered(plan, plane, tiles):
    if tiles & (tiles - 1):
        held = lax.all_gather(plane, "tile", axis=0, tiled=True)
        return chip_rows(plan, held, lax.axis_index("tile") // 2)
    tile, size, held = lax.axis_index("tile"), 1, plane
    while size < tiles:
        taken = lax.ppermute(held, "tile", [(t, t ^ (2 * size - 1)) for t in range(tiles)])
        held = in_order((tile // size) % 2 == 1, held, taken)
        size *= 2
    return chip_rows(plan, held, tile // 2)


def some_planes(planes, tile):
    begin = (jnp.where(faces_lower(tile), planes.shape[0] - 3, 0), 0, 0)
    return lax.dynamic_slice(planes, begin, (3, *planes.shape[1:]))


def even_first(width):
    row = lax.broadcasted_iota(jnp.int32, (width, width), 0)
    col = lax.broadcasted_iota(jnp.int32, (width, width), 1)
    return ones_where(row == 2 * lax.rem(col, width // 2) + lax.div(col, width // 2))


def pair_kernel(plan, plane, taken, mine, theirs):
    tile = lax.axis_index("tile")
    upper, second = lax.rem(tile, 2) == 1, tile >= 2
    order = even_first(plane.shape[2])
    inside = plan.span - plan.rim
    edge = jnp.zeros((plan.rim, plane.shape[2]), F32)
    here, there = (jnp.dot(ref[0].astype(BF), order, preferred_element_type=F32) for ref in (plane, taken))
    for p, rows in enumerate((jnp.where(upper, there, here), jnp.where(upper, here, there))):
        top = jnp.concatenate([edge, rows[:inside]], axis=0)
        bottom = jnp.concatenate([rows[rows.shape[0] - inside :], edge], axis=0)
        mine[p] = jnp.where(second, bottom, top).astype(BF)
        theirs[p] = jnp.where(second, top, bottom).astype(BF)


def exchanged(plan, plane, groups, tiles, weights, make_bands):
    axes, tile = ("freq", "tile"), lax.axis_index("tile")
    if tiles != 4:
        planes = jnp.einsum("pyx,xw->pyw", plane.astype(BF), even_first(plane.shape[2]), preferred_element_type=F32)
        own = gathered(plan, planes.astype(BF), tiles)
        message = some_planes(own, tile + 1)
        return own, lax.ppermute(message, axes, freq_pairs(groups, tiles, 1)), make_bands(weights)
    taken = lax.ppermute(plane, "tile", [(t, t ^ 1) for t in range(tiles)])
    window = jax.ShapeDtypeStruct((2, plan.span, plane.shape[2]), BF)
    mine, theirs = pl.pallas_call(
        functools.partial(pair_kernel, plan),
        name="pair",
        out_shape=[window] * 2,
        in_specs=[VM] * 2,
        out_specs=[VM] * 2,
        compiler_params=pltpu.CompilerParams(vmem_limit_bytes=32 * 2**20),
    )(plane.astype(BF), taken)
    chip = tile // 2
    ahead = lax.ppermute(mine, axes, freq_pairs(groups, tiles, 1))
    aside = lax.ppermute(theirs, axes, freq_pairs(groups, tiles, 3))
    across = lax.ppermute(theirs, "tile", [(t, t ^ 3) for t in range(tiles)])
    ahead, *weights = lax.optimization_barrier((ahead, *weights))
    bands = make_bands(weights)
    aside, *bands = lax.optimization_barrier((aside, *bands))
    own = in_order(chip == 1, mine, across)
    return own, some_planes(in_order(chip == 1, ahead, aside), tile), bands


def body(sky_cube, kernel_one, bias_one, kernel_two, bias_two, kernel_three, bias_three):
    tiles, groups = lax.axis_size("tile"), lax.axis_size("freq")
    strip = sky_cube.shape[1] // tiles
    depth = tiles * sky_cube.shape[0]
    c1, c2, c3 = (kernel.shape[0] for kernel in (kernel_one, kernel_two, kernel_three))
    plan = Plan(strip, depth, c1, c2, c3)
    tile = lax.axis_index("tile")

    w1 = jnp.transpose(kernel_one[:, 0], (1, 2, 3, 0))
    w2 = jnp.transpose(kernel_two, (2, 3, 4, 0, 1))
    w3 = jnp.transpose(kernel_three, (2, 3, 4, 1, 0))

    params = pltpu.CompilerParams(vmem_limit_bytes=32 * 2**20)

    def make_bands(weights):
        return pl.pallas_call(
            functools.partial(bands_kernel, plan),
            name="bands",
            out_shape=[
                jax.ShapeDtypeStruct((plan.n1, plan.k1), BF),
                jax.ShapeDtypeStruct((3 * plan.out2, plan.k2), BF),
                jax.ShapeDtypeStruct((c1, 128), F32),
                jax.ShapeDtypeStruct((c2, 128), F32),
                jax.ShapeDtypeStruct((c3, plan.r3, 128), F32),
                jax.ShapeDtypeStruct((2, 3 * plan.out3, plan.k3), BF),
            ],
            in_specs=[VM] * 6,
            out_specs=[VM] * 6,
            compiler_params=params,
        )(*weights)

    own, got, weights = exchanged(
        plan, sky_cube, groups, tiles, (bias_one[None], bias_two[None], bias_three[None], w1, w2, w3), make_bands
    )
    t1, t2, b1, b2, b3, t3 = weights
    other = lax.ppermute(got, "tile", [(t, t ^ 1) for t in range(tiles)])
    done, middle = pl.pallas_call(
        functools.partial(early_kernel, plan),
        name="early",
        out_shape=[
            jax.ShapeDtypeStruct((plan.planes2, plan.n2, 128), BF),
            jax.ShapeDtypeStruct((depth - 2, plan.n1, 128), BF),
        ],
        in_specs=[VM] * 6,
        out_specs=[VM] * 2,
        compiler_params=params,
    )(own, got, t1, t2, b1, b2)
    other, done = lax.optimization_barrier((other, done))
    return pl.pallas_call(
        functools.partial(late_kernel, plan),
        name="late",
        out_shape=jax.ShapeDtypeStruct((c3, depth // 2, plan.r3, sky_cube.shape[2] // 2), BF),
        in_specs=[VM] * 10,
        out_specs=VM,
        compiler_params=params,
    )(own, other, middle, done, t1, t2, b1, b2, t3, b3)


def solution(mesh):
    return jax.shard_map(
        body,
        mesh=mesh,
        in_specs=(P(("freq", "tile"), None, None), P(), P(), P(), P(), P(), P()),
        out_specs=P(None, "freq", "tile", None),
        check_vma=False,
    )
```
